512 devices in a mesh: stu: 32 (over y, z_lo, core), item: 16 (over z_hi, x).
Axes of the slice: x: 4, y: 8, z: 8 (z_hi: 4, z_lo: 2; z = z_hi * 2 + z_lo), core: 2. Of those that a mesh axis runs over, the one named last changes fastest.
Arguments:
- attempts: bfloat16 [65536, 12288], P('stu', 'item'), may hold values from -0.5 to 0.5
- item_factor: bfloat16 [12288, 64], P('item'), may hold values from -0.0546875 to 0.0546875
- core_factor: float32 [64, 64], replicated, may hold values from -1 to 1.5
- student_weights: float32 [128, 64], P('stu'), may hold values from 0.3 to 3
- blocks: int32 [32, 4], P('stu'), may hold values from 1 to 8, 16 in all within a row
Outputs:
- item_mttkrp: float32 [12288, 64], P('item')
- shared_mttkrp: float32 [64, 64], replicated
- student_mttkrp: float32 [128, 64], P('stu')
The draws below stay inside these ranges and needn't reach their ends.
Inputs may be any that keep to these rules, and one draw needn't show every extreme that they name: Each row of blocks sums to 16, and some student of each row has exactly 8 blocks.
All inputs are finite; a program needn't handle non-finite values.
Results may differ from the reference program's by a relative error of at most 0.0003.
Values sent between devices are 32-bit elements; how exact they have to be, the bound alone decides.
No kernel may reach another device: no remote copies, remote signals or barrier semaphores. Data moves between devices by JAX's collectives and lax.ppermute only.
A program may use at most 64 MiB of HBM per device.

```python
import math
import jax
import jax.numpy as jnp
import numpy as np
from jax import lax

RANK = 64
ITEMS = 12288
ROWS_DEV = 2048
ROWS = 65536
BLK_DEV = 16
STU_DEV = 4
MOST = 8
STUDENTS = 128
GROUPS = 32
NS_STEPS = 6
N_STU = 32


def draw_core_factor(key, part):
    identity = jnp.eye(RANK, dtype=jnp.float32)
    offdiag = jnp.clip(jax.random.normal(key, (RANK, RANK), jnp.float32), -4.0, 4.0)
    return identity + 0.35 * offdiag / math.sqrt(RANK)


def steps_of(own_key, extent, cuts, low, top_value):
    def one(dim, blocks):
        draws = jax.random.uniform(jax.random.fold_in(jax.random.fold_in(own_key, 6), dim), (blocks,), jnp.float32, low / len(cuts), top_value / len(cuts))
        return jnp.repeat(jnp.exp(draws), extent[dim] // blocks).reshape((-1,) + (1,) * (len(extent) - dim - 1))

    loudness = one(*cuts[0])
    for cut in cuts[1:]:
        loudness = loudness * one(*cut)
    return loudness


def length_profile(number_of, total, limit, slope):
    weights = [(1 << 20) // math.isqrt(rank ** slope) + 1 for rank in range(2, number_of + 1)]
    spare, holding = total - limit - (number_of - 1), [1] * (number_of - 1)
    while spare > 0:
        candidates = [i for i in range(number_of - 1) if holding[i] < limit]
        whole, left = sum([weights[i] for i in candidates]), spare
        for i in candidates:
            addition = min(limit - holding[i], max(1, left * weights[i] // whole), spare)
            holding[i] = holding[i] + addition
            spare = spare - addition
    return np.array([limit] + holding)


def uneven(own_key, count, total, most, lean):
    if count == 2:
        one = jax.random.randint(own_key, (), max(1, total - most), min(most, total - 1) + 1)
        return jnp.stack([one, total - one])
    lengths = jnp.asarray(length_profile(count, total, most, lean), jnp.int32)
    couples = (count - 1) // 2
    donor, taker = lengths[1:1 + 2 * couples:2], lengths[2:2 + 2 * couples:2]
    margin = jnp.minimum(donor - 1, most - taker)
    shifted = jax.random.randint(jax.random.fold_in(own_key, 1), (couples,), 0, 1 << 20) % (margin + 1)
    lengths = lengths.at[1:1 + 2 * couples:2].set(donor - shifted).at[2:2 + 2 * couples:2].set(taker + shifted)
    return lengths[jax.random.permutation(jax.random.fold_in(own_key, 2), count)]


def bell_draw(own_key, extent, scale, bound, pieces=(), kind=jnp.bfloat16):
    values = scale * jax.random.normal(own_key, extent, jnp.float32)
    if pieces:
        values = values * steps_of(own_key, extent, pieces, -0.22, 0.18)
    return jnp.clip(values, -bound, bound).astype(kind)


def setup_inputs(seed: int = 0) -> dict:
    keys = jax.random.split(jax.random.key(seed), 6)
    attempts = bell_draw(keys[0], (ROWS, ITEMS), 0.0625, 0.5, ((0, 32), (1, 16)))
    item_factor = bell_draw(keys[1], (ITEMS, RANK), ITEMS ** -0.5, 0.0546875, ((0, 16),))
    core_factor = draw_core_factor(jax.random.fold_in(keys[5], 71), 0)
    student_weights = jnp.clip(jnp.exp(math.log(3.0) - 2.3025851 * jax.random.uniform(keys[3], (STUDENTS, RANK), jnp.float32) ** steps_of(keys[3], (STUDENTS, RANK), ((0, 32),), -0.2, 0.2)), 0.3, 3.0)
    blocks = jax.vmap(lambda own: uneven(own, STU_DEV, BLK_DEV, MOST, 2))(jax.random.split(keys[4], GROUPS)).reshape((GROUPS, STU_DEV)).astype(jnp.int32)
    return {"attempts": attempts, "item_factor": item_factor, "core_factor": core_factor, "student_weights": student_weights, "blocks": blocks}


HIGHEST = lax.Precision.HIGHEST

def owner_table(counts, offset, row_total, group_rows):
    end_rows = jnp.cumsum(counts) * 128
    start_rows = end_rows - counts * 128
    places = offset + jnp.arange(row_total // group_rows, dtype=jnp.int32) * group_rows
    inside = (places[:, None] >= start_rows[None, :]) & (places[:, None] < end_rows[None, :])
    return inside.astype(jnp.float32)

def polar_factor(target, owners, group_rows):
    row_total, width = target.shape
    blocked = target.reshape(row_total // group_rows, group_rows, width)
    identity = jnp.eye(width, dtype=jnp.float32)

    def student_gram(blocked_now):
        grams = jnp.einsum('gla,glb->gab', blocked_now, blocked_now, precision=HIGHEST)
        return jnp.einsum('gk,gab->kab', owners, grams, precision=HIGHEST)
    gram_now = student_gram(blocked)
    diagonal_sum = lax.optimization_barrier(jnp.sum(gram_now * identity, axis=(1, 2)))
    inverse_norm = 1.0 / jnp.sqrt(diagonal_sum + 1e-06)
    blocked = blocked * jnp.dot(owners, inverse_norm, precision=HIGHEST)[:, None, None]
    gram_now = gram_now * (inverse_norm * inverse_norm)[:, None, None]
    for iteration in range(NS_STEPS):
        if iteration > 0:
            gram_now = student_gram(blocked)
        factor = 1.5 * identity - 0.5 * gram_now
        spread = jnp.einsum('gk,kab->gab', owners, factor, precision=HIGHEST)
        blocked = jnp.einsum('gla,gab->glb', blocked, spread, precision=HIGHEST)
    return blocked.reshape(row_total, width)

def student_cross(orthogonal, raw_sums, owners, group_rows):
    row_total, width = raw_sums.shape
    left_side = orthogonal.reshape(row_total // group_rows, group_rows, width)
    right_side = raw_sums.reshape(row_total // group_rows, group_rows, width)
    grams = jnp.einsum('gla,glb->gab', left_side, right_side, precision=HIGHEST)
    return jnp.einsum('gk,gab->kab', owners, grams, precision=HIGHEST)

def scaled_target(raw_sums, owners, group_rows, weights_here, core_factor):
    row_total, width = raw_sums.shape
    row_scale = jnp.dot(owners, weights_here, precision=HIGHEST)
    scaled = raw_sums.reshape(row_total // group_rows, group_rows, width) * row_scale[:, None, :]
    return jnp.dot(scaled.reshape(row_total, width), core_factor.T, precision=HIGHEST)

def reference(attempts, item_factor, core_factor, student_weights, blocks):

    def per_group(carry, group_index):
        item_sum, shared_sum = carry
        rows_here = lax.dynamic_slice_in_dim(attempts, group_index * ROWS_DEV, ROWS_DEV, 0)
        weights_here = lax.dynamic_slice_in_dim(student_weights, group_index * STU_DEV, STU_DEV, 0)
        counts = blocks[group_index]
        owners = owner_table(counts, 0, ROWS_DEV, 128)
        raw_sums = jnp.dot(rows_here, item_factor, preferred_element_type=jnp.float32)
        target = scaled_target(raw_sums, owners, 128, weights_here, core_factor)
        orthogonal = polar_factor(target, owners, 128)
        crossed = student_cross(orthogonal, raw_sums, owners, 128)
        row_scale = jnp.dot(owners, weights_here, precision=HIGHEST)
        lifted = jnp.dot(orthogonal, core_factor, precision=HIGHEST)
        lifted = lifted.reshape(ROWS_DEV // 128, 128, RANK) * row_scale[:, None, :]
        weighted = lifted.reshape(ROWS_DEV, RANK).astype(jnp.bfloat16)
        item_part = lax.dot_general(rows_here, weighted, (((0,), (0,)), ((), ())), preferred_element_type=jnp.float32)
        shared_part = jnp.einsum('kab,kb->ab', crossed, weights_here, precision=HIGHEST)
        student_part = jnp.einsum('ab,kab->kb', core_factor, crossed, precision=HIGHEST)
        return ((item_sum + item_part, shared_sum + shared_part), student_part)
    initial = (jnp.zeros((ITEMS, RANK), jnp.float32), jnp.zeros((RANK, RANK), jnp.float32))
    totals, parts = lax.scan(per_group, initial, jnp.arange(N_STU, dtype=jnp.int32))
    return (totals[0], totals[1], parts.reshape(STUDENTS, RANK))
```

```python
import functools

import jax
import jax.numpy as jnp
from jax import lax
from jax.experimental import pallas as pl
from jax.experimental.pallas import tpu as pltpu
from jax.sharding import PartitionSpec as P

NS_STEPS = 6
BLOCK = 128
F32 = jnp.float32
BF16 = jnp.bfloat16
NN = (((1,), (0,)), ((), ()))
NT = (((1,), (1,)), ((), ()))
VMEM = pl.BlockSpec(memory_space=pltpu.VMEM)
SMEM = pl.BlockSpec(memory_space=pltpu.SMEM)


def project_kernel(factor_ref, rows_ref, out_ref):
    product = lax.dot_general(factor_ref[...], rows_ref[...], NT, preferred_element_type=F32)
    for piece in range(out_ref.shape[0]):
        out_ref[piece] = product[:, piece * BLOCK : (piece + 1) * BLOCK]


def project(attempts, factor_t, blocks_step):
    row_total, items = attempts.shape
    rank = factor_t.shape[0]
    count = row_total // BLOCK
    return pl.pallas_call(
        project_kernel,
        grid=(count // blocks_step,),
        in_specs=[
            pl.BlockSpec((rank, items), lambda i: (0, 0)),
            pl.BlockSpec((blocks_step * BLOCK, items), lambda i: (i, 0)),
        ],
        out_specs=pl.BlockSpec((blocks_step, rank, BLOCK), lambda i: (i, 0, 0)),
        out_shape=jax.ShapeDtypeStruct((count, rank, BLOCK), F32),
        name="project",
    )(factor_t, attempts)


def add_kernel(in_ref, out_ref):
    total = in_ref[0]
    for part in range(1, in_ref.shape[0]):
        total = total + in_ref[part]
    for part in range(out_ref.shape[0]):
        out_ref[part] = total


def add_and_copy(parts, name):
    return pl.pallas_call(
        add_kernel,
        in_specs=[VMEM],
        out_specs=VMEM,
        out_shape=jax.ShapeDtypeStruct(parts.shape, F32),
        name=name,
    )(parts)


def split(value):
    high = value.astype(BF16)
    return high, (value - high.astype(F32)).astype(BF16)


def dot3(left, right_parts, dims):
    rows = left.shape[0]
    high, low = split(left)
    right_high, right_low = right_parts
    both = lax.dot_general(
        jnp.concatenate([high, low], axis=0), right_high, dims, preferred_element_type=F32
    )
    cross = lax.dot_general(high, right_low, dims, preferred_element_type=F32)
    return both[:rows] + (both[rows:] + cross)


def solve_kernel(
    raw_ref, core_ref, weights_ref, counts_ref, attempts_ref,
    parts_ref, student_ref, spread_high, spread_low, held, arrived,
):
    count, rank, _ = raw_ref.shape
    students = weights_ref.shape[0]
    wide = students * rank
    load = pltpu.make_async_copy(attempts_ref, held, arrived)
    load.start()

    ends = [counts_ref[0, 0]]
    for student in range(1, students - 1):
        ends.append(ends[-1] + counts_ref[0, student])
    highs, lows = [], []
    for block in range(count):
        owner = sum((block >= end).astype(jnp.int32) for end in ends)
        value = raw_ref[block]
        high = value.astype(BF16).astype(F32)
        low = value - high
        highs.append(high.astype(BF16))
        lows.append(low.astype(BF16))
        for student in range(students):
            mine = (owner == student).astype(F32)
            place = (pl.ds(student * rank, rank), pl.ds(block * BLOCK, BLOCK))
            spread_high[place] = (high * mine).astype(BF16)
            spread_low[place] = (low * mine).astype(BF16)
    all_high = jnp.concatenate(highs, axis=1)
    all_low = jnp.concatenate(lows, axis=1)

    row_id = lax.broadcasted_iota(jnp.int32, (rank, wide), 0)
    col_id = lax.broadcasted_iota(jnp.int32, (rank, wide), 1)
    identity = (row_id == col_id % rank).astype(F32)
    student_id = col_id // rank
    on_diagonal = (
        lax.broadcasted_iota(jnp.int32, (wide, wide), 0) // rank
        == lax.broadcasted_iota(jnp.int32, (wide, wide), 1) // rank
    ).astype(F32)

    def diagonal(value):
        high = value.astype(BF16).astype(F32)
        low = value - high
        return tuple(
            (jnp.concatenate([half] * students, axis=0) * on_diagonal).astype(BF16)
            for half in (high, low)
        )

    both = lax.dot_general(
        jnp.concatenate([all_high, all_low], axis=0), spread_high[...], NT, preferred_element_type=F32
    )
    cross_term = lax.dot_general(all_high, spread_low[...], NT, preferred_element_type=F32)
    raw_gram = both[:rank] + (both[rank:] + cross_term)

    core = core_ref[...]
    scaled = [core * weights_ref[student : student + 1, :] for student in range(students)]
    lift = jnp.concatenate(scaled, axis=1)
    lift_t = jnp.concatenate([one.T for one in scaled], axis=1)
    lift_diagonal = diagonal(lift)

    half_way = dot3(lift, diagonal(raw_gram), NN)
    gram = dot3(half_way, lift_diagonal, NT)
    trace_row = jnp.sum(gram * identity, axis=0, keepdims=True)
    inverse = jnp.zeros((1, wide), F32)
    lane_student = student_id[:1]
    for student in range(students):
        here = lane_student == student
        trace = jnp.sum(jnp.where(here, trace_row, 0.0), axis=1, keepdims=True)
        inverse = jnp.where(here, 1.0 / jnp.sqrt(trace + 1e-06), inverse)
    gram = gram * (inverse * inverse)
    polynomial = None
    for iteration in range(NS_STEPS):
        factor = 1.5 * identity - 0.5 * gram
        factor_diagonal = diagonal(factor)
        last = iteration == NS_STEPS - 1
        if iteration == 0:
            moved = dot3(gram, factor_diagonal, NN)
            polynomial = factor
        elif last:
            polynomial = dot3(polynomial, factor_diagonal, NN)
        else:
            pair = dot3(jnp.concatenate([gram, polynomial], axis=0), factor_diagonal, NN)
            moved, polynomial = pair[:rank], pair[rank:]
        if not last:
            gram = dot3(moved, factor_diagonal, NN)
    polynomial = polynomial * inverse

    crossed = dot3(polynomial, diagonal(half_way), NN)
    lifted = dot3(polynomial, lift_diagonal, NN)
    apply = dot3(lift_t, diagonal(lifted), NN)

    shared = jnp.zeros((rank, rank), F32)
    for student in range(students):
        one = crossed[:, student * rank : (student + 1) * rank]
        shared = shared + one * weights_ref[student : student + 1, :]
        student_ref[student : student + 1, :] = jnp.sum(one * core, axis=0, keepdims=True)

    weighted = dot3(apply, (spread_high[...], spread_low[...]), NN).astype(BF16)
    load.wait()
    item_part = jnp.dot(weighted, held[...], preferred_element_type=F32)
    tiles = item_part.shape[1] // BLOCK
    for tile in range(tiles):
        parts_ref[tile * rank : (tile + 1) * rank, :] = item_part[:, tile * BLOCK : (tile + 1) * BLOCK]
    parts_ref[tiles * rank :, :] = jnp.zeros((parts_ref.shape[0] - tiles * rank, BLOCK), F32)
    parts_ref[tiles * rank : (tiles + 1) * rank, :rank] = shared


def solve(raw, core_factor, student_weights, blocks, attempts, part_rows):
    count, rank, _ = raw.shape
    students = student_weights.shape[0]
    wide = (students * rank, count * BLOCK)
    return pl.pallas_call(
        solve_kernel,
        in_specs=[VMEM, VMEM, VMEM, SMEM, pl.BlockSpec(memory_space=pl.ANY)],
        out_specs=[VMEM, VMEM],
        out_shape=[
            jax.ShapeDtypeStruct((part_rows, BLOCK), F32),
            jax.ShapeDtypeStruct((students, rank), F32),
        ],
        scratch_shapes=[
            pltpu.VMEM(wide, BF16),
            pltpu.VMEM(wide, BF16),
            pltpu.VMEM(attempts.shape, BF16),
            pltpu.SemaphoreType.DMA,
        ],
        compiler_params=pltpu.CompilerParams(vmem_limit_bytes=32 * 1024 * 1024),
        name="solve",
    )(raw, core_factor, student_weights, blocks, attempts)


def exchange(parts, axis):
    return lax.all_to_all(parts, axis, 0, 0, tiled=True)


def local(n_stu, attempts, item_factor, core_factor, student_weights, blocks):
    items, rank = item_factor.shape
    sums = project(attempts, item_factor.T, 4)
    sums = exchange(sums, "item")
    raw = exchange(add_and_copy(sums, "add_item"), "item")
    tiles = items // BLOCK
    step = 8 * n_stu
    part_rows = -(-(tiles + 1) * rank // step) * step
    parts, student_part = solve(raw, core_factor, student_weights, blocks, attempts, part_rows)
    parts = exchange(parts.reshape(n_stu, part_rows // n_stu, BLOCK), "stu")
    total = exchange(add_and_copy(parts, "add_stu"), "stu").reshape(part_rows, BLOCK)
    item_total = total[: tiles * rank].reshape(tiles, rank, BLOCK).transpose(1, 0, 2)
    shared_total = total[tiles * rank : (tiles + 1) * rank, :rank]
    return (item_total.reshape(rank, items).T, shared_total, student_part)


def solution(mesh):
    in_specs = (P("stu", "item"), P("item", None), P(), P("stu", None), P("stu", None))
    out_specs = (P("item", None), P(), P("stu", None))
    body = functools.partial(local, mesh.shape["stu"])
    return jax.shard_map(body, mesh=mesh, in_specs=in_specs, out_specs=out_specs, check_vma=False)
```

```python
import functools

import jax
import jax.numpy as jnp
from jax import lax
from jax.experimental import pallas as pl
from jax.experimental.pallas import tpu as pltpu
from jax.sharding import PartitionSpec as P

NS_STEPS = 6
BLOCK = 128
NEAR = 4
F32 = jnp.float32
BF16 = jnp.bfloat16
NN = (((1,), (0,)), ((), ()))
NT = (((1,), (1,)), ((), ()))
VMEM = pl.BlockSpec(memory_space=pltpu.VMEM)
SMEM = pl.BlockSpec(memory_space=pltpu.SMEM)


def project(attempts, factor_t):
    row_total, items = attempts.shape
    blocked = attempts.reshape(row_total // BLOCK, BLOCK, items)
    return jnp.einsum("ri,bli->brl", factor_t, blocked, preferred_element_type=F32)


def add_kernel(in_ref, out_ref):
    total = in_ref[0]
    for part in range(1, in_ref.shape[0]):
        total = total + in_ref[part]
    for part in range(out_ref.shape[0]):
        out_ref[part] = total


def add_and_copy(parts, copies, name):
    return pl.pallas_call(
        add_kernel,
        in_specs=[VMEM],
        out_specs=VMEM,
        out_shape=jax.ShapeDtypeStruct((copies, *parts.shape[1:]), F32),
        compiler_params=pltpu.CompilerParams(vmem_limit_bytes=2 * parts.size * 4 + 1024 * 1024),
        name=name,
    )(parts)


def split(value):
    high = value.astype(BF16)
    return high, (value - high.astype(F32)).astype(BF16)


def dot3(left, right_parts, dims):
    rows = left.shape[0]
    high, low = split(left)
    right_high, right_low = right_parts
    both = lax.dot_general(
        jnp.concatenate([high, low], axis=0), right_high, dims, preferred_element_type=F32
    )
    cross = lax.dot_general(high, right_low, dims, preferred_element_type=F32)
    return both[:rows] + (both[rows:] + cross)


def solve_kernel(
    raw_ref, core_ref, weights_ref, counts_ref, attempts_ref,
    parts_ref, student_ref, spread_high, spread_low, held, arrived,
):
    count, rank, _ = raw_ref.shape
    students = weights_ref.shape[0]
    wide = students * rank
    load = pltpu.make_async_copy(attempts_ref, held, arrived)
    load.start()

    ends = [counts_ref[0, 0]]
    for student in range(1, students - 1):
        ends.append(ends[-1] + counts_ref[0, student])
    highs, lows = [], []
    for block in range(count):
        owner = sum((block >= end).astype(jnp.int32) for end in ends)
        value = raw_ref[block]
        high = value.astype(BF16).astype(F32)
        low = value - high
        highs.append(high.astype(BF16))
        lows.append(low.astype(BF16))
        for student in range(students):
            mine = (owner == student).astype(F32)
            place = (pl.ds(student * rank, rank), pl.ds(block * BLOCK, BLOCK))
            spread_high[place] = (high * mine).astype(BF16)
            spread_low[place] = (low * mine).astype(BF16)
    all_high = jnp.concatenate(highs, axis=1)
    all_low = jnp.concatenate(lows, axis=1)

    row_id = lax.broadcasted_iota(jnp.int32, (rank, wide), 0)
    col_id = lax.broadcasted_iota(jnp.int32, (rank, wide), 1)
    identity = (row_id == col_id % rank).astype(F32)
    student_id = col_id // rank
    on_diagonal = (
        lax.broadcasted_iota(jnp.int32, (wide, wide), 0) // rank
        == lax.broadcasted_iota(jnp.int32, (wide, wide), 1) // rank
    ).astype(F32)

    def diagonal(value):
        high = value.astype(BF16).astype(F32)
        low = value - high
        return tuple(
            (jnp.concatenate([half] * students, axis=0) * on_diagonal).astype(BF16)
            for half in (high, low)
        )

    both = lax.dot_general(
        jnp.concatenate([all_high, all_low], axis=0), spread_high[...], NT, preferred_element_type=F32
    )
    cross_term = lax.dot_general(all_high, spread_low[...], NT, preferred_element_type=F32)
    raw_gram = both[:rank] + (both[rank:] + cross_term)

    core = core_ref[...]
    scaled = [core * weights_ref[student : student + 1, :] for student in range(students)]
    lift = jnp.concatenate(scaled, axis=1)
    lift_t = jnp.concatenate([one.T for one in scaled], axis=1)
    lift_diagonal = diagonal(lift)

    half_way = dot3(lift, diagonal(raw_gram), NN)
    gram = dot3(half_way, lift_diagonal, NT)
    trace_row = jnp.sum(gram * identity, axis=0, keepdims=True)
    inverse = jnp.zeros((1, wide), F32)
    lane_student = student_id[:1]
    for student in range(students):
        here = lane_student == student
        trace = jnp.sum(jnp.where(here, trace_row, 0.0), axis=1, keepdims=True)
        inverse = jnp.where(here, 1.0 / jnp.sqrt(trace + 1e-06), inverse)
    gram = gram * (inverse * inverse)
    polynomial = None
    for iteration in range(NS_STEPS):
        factor = 1.5 * identity - 0.5 * gram
        factor_diagonal = diagonal(factor)
        last = iteration == NS_STEPS - 1
        if iteration == 0:
            moved = dot3(gram, factor_diagonal, NN)
            polynomial = factor
        elif last:
            polynomial = dot3(polynomial, factor_diagonal, NN)
        else:
            pair = dot3(jnp.concatenate([gram, polynomial], axis=0), factor_diagonal, NN)
            moved, polynomial = pair[:rank], pair[rank:]
        if not last:
            gram = dot3(moved, factor_diagonal, NN)
    polynomial = polynomial * inverse

    crossed = dot3(polynomial, diagonal(half_way), NN)
    lifted = dot3(polynomial, lift_diagonal, NN)
    apply = dot3(lift_t, diagonal(lifted), NN)

    shared = jnp.zeros((rank, rank), F32)
    for student in range(students):
        one = crossed[:, student * rank : (student + 1) * rank]
        shared = shared + one * weights_ref[student : student + 1, :]
        student_ref[student : student + 1, :] = jnp.sum(one * core, axis=0, keepdims=True)

    weighted = dot3(apply, (spread_high[...], spread_low[...]), NN).astype(BF16)
    load.wait()
    item_part = jnp.dot(weighted, held[...], preferred_element_type=F32)
    tiles = item_part.shape[1] // BLOCK
    for tile in range(tiles):
        parts_ref[tile * rank : (tile + 1) * rank, :] = item_part[:, tile * BLOCK : (tile + 1) * BLOCK]
    parts_ref[tiles * rank :, :] = jnp.zeros((parts_ref.shape[0] - tiles * rank, BLOCK), F32)
    parts_ref[tiles * rank : (tiles + 1) * rank, :rank] = shared


def solve(raw, core_factor, student_weights, blocks, attempts, part_rows):
    count, rank, _ = raw.shape
    students = student_weights.shape[0]
    wide = (students * rank, count * BLOCK)
    return pl.pallas_call(
        solve_kernel,
        in_specs=[VMEM, VMEM, VMEM, SMEM, pl.BlockSpec(memory_space=pl.ANY)],
        out_specs=[VMEM, VMEM],
        out_shape=[
            jax.ShapeDtypeStruct((part_rows, BLOCK), F32),
            jax.ShapeDtypeStruct((students, rank), F32),
        ],
        scratch_shapes=[
            pltpu.VMEM(wide, BF16),
            pltpu.VMEM(wide, BF16),
            pltpu.VMEM(attempts.shape, BF16),
            pltpu.SemaphoreType.DMA,
        ],
        compiler_params=pltpu.CompilerParams(vmem_limit_bytes=16 * 1024 * 1024),
        name="solve",
    )(raw, core_factor, student_weights, blocks, attempts)


def exchange(parts, axis, groups=None):
    return lax.all_to_all(parts, axis, 0, 0, tiled=True, axis_index_groups=groups)


def sum_over_item(parts, n_item):
    near = [[far * NEAR + i for i in range(NEAR)] for far in range(n_item // NEAR)]
    distant = [[far * NEAR + i for far in range(n_item // NEAR)] for i in range(NEAR)]
    shares = parts.reshape(NEAR, -1, BLOCK)
    shares = exchange(shares, "item", near)
    shares = exchange(add_and_copy(shares, n_item // NEAR, "add_near"), "item", distant)
    shares = exchange(add_and_copy(shares, NEAR, "add_far"), "item", near)
    return shares.reshape(parts.shape)


def local(n_stu, n_item, attempts, item_factor, core_factor, student_weights, blocks):
    items, rank = item_factor.shape
    raw = sum_over_item(project(attempts, item_factor.T), n_item)
    tiles = items // BLOCK
    step = 8 * n_stu
    part_rows = -(-(tiles + 1) * rank // step) * step
    parts, student_part = solve(raw, core_factor, student_weights, blocks, attempts, part_rows)
    parts = exchange(parts.reshape(n_stu, part_rows // n_stu, BLOCK), "stu")
    total = exchange(add_and_copy(parts, n_stu, "add_stu"), "stu").reshape(part_rows, BLOCK)
    item_total = total[: tiles * rank].reshape(tiles, rank, BLOCK).transpose(1, 0, 2)
    shared_total = total[tiles * rank : (tiles + 1) * rank, :rank]
    return (item_total.reshape(rank, items).T, shared_total, student_part)


def solution(mesh):
    in_specs = (P("stu", "item"), P("item", None), P(), P("stu", None), P("stu", None))
    out_specs = (P("item", None), P(), P("stu", None))
    body = functools.partial(local, mesh.shape["stu"], mesh.shape["item"])
    return jax.shard_map(body, mesh=mesh, in_specs=in_specs, out_specs=out_specs, check_vma=False)
```

```python
import functools

import jax
import jax.numpy as jnp
from jax import lax
from jax.experimental import pallas as pl
from jax.experimental.pallas import tpu as pltpu
from jax.sharding import PartitionSpec as P

NS_STEPS = 6
PROJECT_VMEM = 56 * 1024 * 1024
BLOCK = 128
NEAR = 4
F32 = jnp.float32
BF16 = jnp.bfloat16
NN = (((1,), (0,)), ((), ()))
NT = (((1,), (1,)), ((), ()))
VMEM = pl.BlockSpec(memory_space=pltpu.VMEM)
SMEM = pl.BlockSpec(memory_space=pltpu.SMEM)


def project_kernel(factor_ref, rows_ref, out_ref, factor, held, arrived, factor_arrived):
    chunks = arrived.shape[0]
    rows = held.shape[0] // chunks
    factor_load = pltpu.make_async_copy(factor_ref, factor, factor_arrived)
    factor_load.start()
    loads = []
    for chunk in range(chunks):
        place = pl.ds(chunk * rows, rows)
        loads.append(pltpu.make_async_copy(rows_ref.at[place], held.at[place], arrived.at[chunk]))
        loads[-1].start()
    factor_load.wait()
    pieces = rows // BLOCK
    for chunk in range(chunks):
        loads[chunk].wait()
        here = held[chunk * rows : (chunk + 1) * rows, :]
        product = lax.dot_general(factor[...], here, NT, preferred_element_type=F32)
        for piece in range(pieces):
            out_ref[chunk * pieces + piece] = product[:, piece * BLOCK : (piece + 1) * BLOCK]


def project(attempts, factor_t, chunks):
    row_total, items = attempts.shape
    rank = factor_t.shape[0]
    return pl.pallas_call(
        project_kernel,
        in_specs=[pl.BlockSpec(memory_space=pl.ANY)] * 2,
        out_specs=VMEM,
        out_shape=pltpu.VMEM((row_total // BLOCK, rank, BLOCK), F32),
        scratch_shapes=[
            pltpu.VMEM(factor_t.shape, BF16),
            pltpu.VMEM(attempts.shape, BF16),
            pltpu.SemaphoreType.DMA((chunks,)),
            pltpu.SemaphoreType.DMA,
        ],
        compiler_params=pltpu.CompilerParams(vmem_limit_bytes=PROJECT_VMEM),
        name="project",
    )(factor_t, attempts)


def add_kernel(in_ref, out_ref):
    total = in_ref[0]
    for part in range(1, in_ref.shape[0]):
        total = total + in_ref[part]
    for part in range(out_ref.shape[0]):
        out_ref[part] = total


def add_and_copy(parts, copies, name):
    return pl.pallas_call(
        add_kernel,
        in_specs=[VMEM],
        out_specs=VMEM,
        out_shape=jax.ShapeDtypeStruct((copies, *parts.shape[1:]), F32),
        compiler_params=pltpu.CompilerParams(vmem_limit_bytes=2 * parts.size * 4 + 1024 * 1024),
        name=name,
    )(parts)


def split(value):
    high = value.astype(BF16)
    return high, (value - high.astype(F32)).astype(BF16)


def dot3(left, right_parts, dims):
    rows = left.shape[0]
    high, low = split(left)
    right_high, right_low = right_parts
    both = lax.dot_general(
        jnp.concatenate([high, low], axis=0), right_high, dims, preferred_element_type=F32
    )
    cross = lax.dot_general(high, right_low, dims, preferred_element_type=F32)
    return both[:rows] + (both[rows:] + cross)


def solve_kernel(
    raw_ref, core_ref, weights_ref, counts_ref, attempts_ref,
    parts_ref, student_ref, halves, grams, lifts,
):
    count, rank, _ = raw_ref.shape
    students = weights_ref.shape[0]
    wide = students * rank

    ends = [counts_ref[0, 0]]
    for student in range(1, students - 1):
        ends.append(ends[-1] + counts_ref[0, student])
    owners = [sum((block >= end).astype(jnp.int32) for end in ends) for block in range(count)]
    grams[...] = jnp.zeros(grams.shape, F32)
    for block in range(count):
        both = jnp.concatenate(split(raw_ref[block]), axis=0)
        halves[block] = both
        grams[owners[block]] += lax.dot_general(both, both, NT, preferred_element_type=F32)

    row_id = lax.broadcasted_iota(jnp.int32, (rank, wide), 0)
    col_id = lax.broadcasted_iota(jnp.int32, (rank, wide), 1)
    identity = (row_id == col_id % rank).astype(F32)
    student_id = col_id // rank
    on_diagonal = (
        lax.broadcasted_iota(jnp.int32, (wide, wide), 0) // rank
        == lax.broadcasted_iota(jnp.int32, (wide, wide), 1) // rank
    ).astype(F32)

    def diagonal(value):
        high = value.astype(BF16).astype(F32)
        low = value - high
        return tuple(
            (jnp.concatenate([half] * students, axis=0) * on_diagonal).astype(BF16)
            for half in (high, low)
        )

    def beside(parts):
        return jnp.concatenate(parts, axis=1)

    core = core_ref[...]
    scaled = [core * weights_ref[student : student + 1, :] for student in range(students)]
    lift_t = beside([one.T for one in scaled])
    lift_diagonal = diagonal(beside(scaled))

    raw_grams = []
    for student in range(students):
        terms = grams[student]
        rows = terms[:rank] + terms[rank:]
        raw_grams.append(rows[:, :rank] + rows[:, rank:])
    raw_diagonal = diagonal(beside(raw_grams))
    gram = dot3(dot3(beside(scaled), raw_diagonal, NN), lift_diagonal, NT)
    trace_row = jnp.sum(gram * identity, axis=0, keepdims=True)
    inverse = jnp.zeros((1, wide), F32)
    lane_student = student_id[:1]
    for student in range(students):
        here = lane_student == student
        trace = jnp.sum(jnp.where(here, trace_row, 0.0), axis=1, keepdims=True)
        inverse = jnp.where(here, 1.0 / jnp.sqrt(trace + 1e-06), inverse)
    gram = gram * (inverse * inverse)
    polynomial = lift_t * inverse
    for iteration in range(NS_STEPS):
        factor_diagonal = diagonal(1.5 * identity - 0.5 * gram)
        if iteration == NS_STEPS - 1:
            polynomial = dot3(polynomial, factor_diagonal, NN)
        else:
            pair = dot3(jnp.concatenate([gram, polynomial], axis=0), factor_diagonal, NN)
            polynomial = pair[rank:]
            gram = dot3(pair[:rank], factor_diagonal, NN)

    apply = dot3(polynomial, lift_diagonal, NN)
    for student in range(students):
        high, low = split(apply[:, student * rank : (student + 1) * rank])
        lifts[student] = jnp.concatenate([beside([high, high]), beside([low, low])], axis=0)
    weighted = []
    for block in range(count):
        terms = jnp.dot(lifts[owners[block]], halves[block], preferred_element_type=F32)
        weighted.append((terms[:rank] + terms[rank:]).astype(BF16))
    item_part = jnp.dot(beside(weighted), attempts_ref[...], preferred_element_type=F32)

    turned = beside([polynomial[:, k * rank : (k + 1) * rank].T for k in range(students)])
    crossed = dot3(turned, raw_diagonal, NN)
    shared = jnp.zeros((rank, rank), F32)
    for student in range(students):
        one = crossed[:, student * rank : (student + 1) * rank]
        shared = shared + one * weights_ref[student : student + 1, :]
        student_ref[student : student + 1, :] = jnp.sum(one * core, axis=0, keepdims=True)

    tiles = item_part.shape[1] // BLOCK
    for tile in range(tiles):
        parts_ref[tile * rank : (tile + 1) * rank, :] = item_part[:, tile * BLOCK : (tile + 1) * BLOCK]
    parts_ref[tiles * rank :, :] = jnp.zeros((parts_ref.shape[0] - tiles * rank, BLOCK), F32)
    parts_ref[tiles * rank : (tiles + 1) * rank, :rank] = shared


def solve(raw, core_factor, student_weights, blocks, attempts, part_rows):
    count, rank, _ = raw.shape
    students = student_weights.shape[0]
    return pl.pallas_call(
        solve_kernel,
        in_specs=[VMEM, VMEM, VMEM, SMEM, VMEM],
        out_specs=[VMEM, VMEM],
        out_shape=[
            jax.ShapeDtypeStruct((part_rows, BLOCK), F32),
            jax.ShapeDtypeStruct((students, rank), F32),
        ],
        scratch_shapes=[
            pltpu.VMEM((count, 2 * rank, BLOCK), BF16),
            pltpu.VMEM((students, 2 * rank, 2 * rank), F32),
            pltpu.VMEM((students, 2 * rank, 2 * rank), BF16),
        ],
        compiler_params=pltpu.CompilerParams(vmem_limit_bytes=16 * 1024 * 1024),
        name="solve",
    )(raw, core_factor, student_weights, blocks, attempts)


def finish_kernel(total_ref, item_ref, shared_ref):
    rank, items = item_ref.shape
    for tile in range(items // BLOCK):
        item_ref[:, tile * BLOCK : (tile + 1) * BLOCK] = total_ref[tile * rank : (tile + 1) * rank, :]
    last = items // BLOCK * rank
    shared_ref[...] = total_ref[last : last + rank, :rank]


def finish(total, rank, items):
    return pl.pallas_call(
        finish_kernel,
        in_specs=[VMEM],
        out_specs=[VMEM, VMEM],
        out_shape=[
            jax.ShapeDtypeStruct((rank, items), F32),
            jax.ShapeDtypeStruct((rank, rank), F32),
        ],
        compiler_params=pltpu.CompilerParams(vmem_limit_bytes=2 * 1024 * 1024),
        name="finish",
    )(total)


def exchange(parts, axis, groups=None):
    return lax.all_to_all(parts, axis, 0, 0, tiled=True, axis_index_groups=groups)


def sum_over_item(parts, n_item):
    near = [[far * NEAR + i for i in range(NEAR)] for far in range(n_item // NEAR)]
    distant = [[far * NEAR + i for far in range(n_item // NEAR)] for i in range(NEAR)]
    shares = parts.reshape(NEAR, -1, BLOCK)
    shares = exchange(shares, "item", near)
    shares = exchange(add_and_copy(shares, n_item // NEAR, "add_near"), "item", distant)
    shares = exchange(add_and_copy(shares, NEAR, "add_far"), "item", near)
    return shares.reshape(parts.shape)


def local(n_stu, n_item, attempts, item_factor, core_factor, student_weights, blocks):
    items, rank = item_factor.shape
    raw = sum_over_item(project(attempts, item_factor.T, 2), n_item)
    tiles = items // BLOCK
    step = 8 * n_stu
    part_rows = -(-(tiles + 1) * rank // step) * step
    parts, student_part = solve(raw, core_factor, student_weights, blocks, attempts, part_rows)
    parts = exchange(parts.reshape(n_stu, part_rows // n_stu, BLOCK), "stu")
    total = exchange(add_and_copy(parts, n_stu, "add_stu"), "stu").reshape(part_rows, BLOCK)
    item_total, shared_total = finish(total, rank, items)
    return (item_total.T, shared_total, student_part)


def solution(mesh):
    in_specs = (P("stu", "item"), P("item", None), P(), P("stu", None), P("stu", None))
    out_specs = (P("item", None), P(), P("stu", None))
    body = functools.partial(local, mesh.shape["stu"], mesh.shape["item"])
    return jax.shard_map(body, mesh=mesh, in_specs=in_specs, out_specs=out_specs, check_vma=False)
```

```python
import functools

import jax
import jax.numpy as jnp
from jax import lax
from jax.experimental import pallas as pl
from jax.experimental.pallas import tpu as pltpu
from jax.sharding import PartitionSpec as P

NS_STEPS = 6
PROJECT_VMEM = 56 * 1024 * 1024
BLOCK = 128
NEAR = 4
F32 = jnp.float32
BF16 = jnp.bfloat16
NN = (((1,), (0,)), ((), ()))
NT = (((1,), (1,)), ((), ()))
VMEM = pl.BlockSpec(memory_space=pltpu.VMEM)
SMEM = pl.BlockSpec(memory_space=pltpu.SMEM)


def project_kernel(factor_ref, rows_ref, out_ref, factor, held, arrived, factor_arrived):
    chunks = arrived.shape[0]
    rows = held.shape[0] // chunks
    factor_load = pltpu.make_async_copy(factor_ref, factor, factor_arrived)
    factor_load.start()
    loads = []
    for chunk in range(chunks):
        place = pl.ds(chunk * rows, rows)
        loads.append(pltpu.make_async_copy(rows_ref.at[place], held.at[place], arrived.at[chunk]))
        loads[-1].start()
    factor_load.wait()
    pieces = rows // BLOCK
    for chunk in range(chunks):
        loads[chunk].wait()
        here = held[chunk * rows : (chunk + 1) * rows, :]
        product = lax.dot_general(factor[...], here, NT, preferred_element_type=F32)
        for piece in range(pieces):
            out_ref[chunk * pieces + piece] = product[:, piece * BLOCK : (piece + 1) * BLOCK]


def project(attempts, factor_t, chunks):
    row_total, items = attempts.shape
    rank = factor_t.shape[0]
    return pl.pallas_call(
        project_kernel,
        in_specs=[pl.BlockSpec(memory_space=pl.ANY)] * 2,
        out_specs=VMEM,
        out_shape=pltpu.VMEM((row_total // BLOCK, rank, BLOCK), F32),
        scratch_shapes=[
            pltpu.VMEM(factor_t.shape, BF16),
            pltpu.VMEM(attempts.shape, BF16),
            pltpu.SemaphoreType.DMA((chunks,)),
            pltpu.SemaphoreType.DMA,
        ],
        compiler_params=pltpu.CompilerParams(vmem_limit_bytes=PROJECT_VMEM),
        name="project",
    )(factor_t, attempts)


def add_kernel(in_ref, out_ref, *, parts, copies):
    rows = in_ref.shape[0] // parts
    total = in_ref[:rows, :]
    for part in range(1, parts):
        total = total + in_ref[part * rows : (part + 1) * rows, :]
    for copy in range(copies):
        out_ref[copy * rows : (copy + 1) * rows, :] = total


def add_and_copy(rows, parts, copies, name):
    out_shape = (rows.shape[0] // parts * copies, BLOCK)
    return pl.pallas_call(
        functools.partial(add_kernel, parts=parts, copies=copies),
        in_specs=[VMEM],
        out_specs=VMEM,
        out_shape=jax.ShapeDtypeStruct(out_shape, F32),
        compiler_params=pltpu.CompilerParams(vmem_limit_bytes=2 * rows.size * 4 + 1024 * 1024),
        name=name,
    )(rows)


def split(value):
    high = value.astype(BF16)
    return high, (value - high.astype(F32)).astype(BF16)


def right_factor(pair, left_lanes, right_lanes):
    parts = [half * lanes for half in split(pair) for lanes in (left_lanes, right_lanes)]
    return jnp.concatenate(parts, axis=0)


def times(left, right):
    rows = left.shape[0]
    both = jnp.concatenate([jnp.concatenate([half, half], axis=1) for half in split(left)], axis=0)
    product = jnp.dot(both, right, preferred_element_type=F32)
    return product[:rows] + product[rows:]


def solve_kernel(
    raw_ref, core_ref, weights_ref, counts_ref, attempts_ref,
    parts_ref, student_ref, halves, grams, lifts,
):
    count, rank, _ = raw_ref.shape
    students = weights_ref.shape[0]
    wide = students * rank

    ends = [counts_ref[0, 0]]
    for student in range(1, students - 1):
        ends.append(ends[-1] + counts_ref[0, student])
    owners = [sum((block >= end).astype(jnp.int32) for end in ends) for block in range(count)]
    grams[...] = jnp.zeros(grams.shape, F32)
    for block in range(count):
        both = jnp.concatenate(split(raw_ref[block]), axis=0)
        halves[block] = both
        grams[owners[block]] += lax.dot_general(both, both, NT, preferred_element_type=F32)

    lane = lax.broadcasted_iota(jnp.int32, (rank, 2 * rank), 1)
    identity = (lax.broadcasted_iota(jnp.int32, (rank, 2 * rank), 0) == lane % rank).astype(F32)
    on_left = lane[:1] < rank
    left_lanes = (lane < rank).astype(F32).astype(BF16)
    right_lanes = (lane >= rank).astype(F32).astype(BF16)

    def right(pair):
        return right_factor(pair, left_lanes, right_lanes)

    def beside(parts):
        return jnp.concatenate(parts, axis=1)

    core = core_ref[...]
    pairs = range(students // 2)
    scaled = [core * weights_ref[student : student + 1, :] for student in range(students)]
    lift = [beside(scaled[2 * pair : 2 * pair + 2]) for pair in pairs]
    lift_t = [beside([one.T for one in scaled[2 * pair : 2 * pair + 2]]) for pair in pairs]
    lift_right = [right(one) for one in lift]
    lift_t_right = [right(one) for one in lift_t]

    raw_grams = []
    for student in range(students):
        terms = grams[student]
        rows = terms[:rank] + terms[rank:]
        raw_grams.append(rows[:, :rank] + rows[:, rank:])
    raw_right = [right(beside(raw_grams[2 * pair : 2 * pair + 2])) for pair in pairs]
    gram, polynomial = [], []
    for pair in pairs:
        half_way = times(lift[pair], raw_right[pair])
        row = jnp.sum(half_way * lift[pair], axis=0, keepdims=True)
        left_trace = jnp.sum(jnp.where(on_left, row, 0.0), axis=1, keepdims=True)
        right_trace = jnp.sum(jnp.where(on_left, 0.0, row), axis=1, keepdims=True)
        inverse = 1.0 / jnp.sqrt(jnp.where(on_left, left_trace, right_trace) + 1e-06)
        gram.append(times(half_way, lift_t_right[pair]) * (inverse * inverse))
        polynomial.append(lift_t[pair] * inverse)
    for iteration in range(NS_STEPS):
        for pair in pairs:
            factor = right(1.5 * identity - 0.5 * gram[pair])
            if iteration == NS_STEPS - 1:
                polynomial[pair] = times(polynomial[pair], factor)
            else:
                moved = times(jnp.concatenate([gram[pair], polynomial[pair]], axis=0), factor)
                polynomial[pair] = moved[rank:]
                gram[pair] = times(moved[:rank], factor)

    apply = beside([times(polynomial[pair], lift_right[pair]) for pair in pairs])
    polynomial = beside(polynomial)
    for student in range(students):
        high, low = split(apply[:, student * rank : (student + 1) * rank])
        lifts[student] = jnp.concatenate([beside([high, high]), beside([low, low])], axis=0)
    weighted = []
    for block in range(count):
        terms = jnp.dot(lifts[owners[block]], halves[block], preferred_element_type=F32)
        weighted.append((terms[:rank] + terms[rank:]).astype(BF16))
    item_part = jnp.dot(beside(weighted), attempts_ref[...], preferred_element_type=F32)

    turned = beside([polynomial[:, k * rank : (k + 1) * rank].T for k in range(students)])
    crossed = beside([times(turned[:, 2 * pair * rank : 2 * (pair + 1) * rank], raw_right[pair]) for pair in pairs])
    shared = jnp.zeros((rank, rank), F32)
    for student in range(students):
        one = crossed[:, student * rank : (student + 1) * rank]
        shared = shared + one * weights_ref[student : student + 1, :]
        student_ref[student : student + 1, :] = jnp.sum(one * core, axis=0, keepdims=True)

    tiles = item_part.shape[1] // BLOCK
    for tile in range(tiles):
        parts_ref[tile * rank : (tile + 1) * rank, :] = item_part[:, tile * BLOCK : (tile + 1) * BLOCK]
    last = tiles * rank
    parts_ref[last : last + rank // 2, :] = beside([shared[: rank // 2], shared[rank // 2 :]])


def solve(raw, core_factor, student_weights, blocks, attempts, part_rows):
    count, rank, _ = raw.shape
    students = student_weights.shape[0]
    return pl.pallas_call(
        solve_kernel,
        in_specs=[VMEM, VMEM, VMEM, SMEM, VMEM],
        out_specs=[VMEM, VMEM],
        out_shape=[
            jax.ShapeDtypeStruct((part_rows, BLOCK), F32),
            jax.ShapeDtypeStruct((students, rank), F32),
        ],
        scratch_shapes=[
            pltpu.VMEM((count, 2 * rank, BLOCK), BF16),
            pltpu.VMEM((students, 2 * rank, 2 * rank), F32),
            pltpu.VMEM((students, 2 * rank, 2 * rank), BF16),
        ],
        compiler_params=pltpu.CompilerParams(vmem_limit_bytes=16 * 1024 * 1024),
        name="solve",
    )(raw, core_factor, student_weights, blocks, attempts)


def finish_kernel(total_ref, item_ref, shared_ref):
    rank, items = item_ref.shape
    for tile in range(items // BLOCK):
        item_ref[:, tile * BLOCK : (tile + 1) * BLOCK] = total_ref[tile * rank : (tile + 1) * rank, :]
    last = items // BLOCK * rank
    both = total_ref[last : last + rank // 2, :]
    shared_ref[: rank // 2, :] = both[:, :rank]
    shared_ref[rank // 2 :, :] = both[:, rank:]


def finish(total, rank, items):
    return pl.pallas_call(
        finish_kernel,
        in_specs=[VMEM],
        out_specs=[VMEM, VMEM],
        out_shape=[
            jax.ShapeDtypeStruct((rank, items), F32),
            jax.ShapeDtypeStruct((rank, rank), F32),
        ],
        compiler_params=pltpu.CompilerParams(vmem_limit_bytes=2 * 1024 * 1024),
        name="finish",
    )(total)


def exchange(rows, parts, axis, groups=None):
    parted = rows.reshape(parts, -1, 1, BLOCK)
    return lax.all_to_all(parted, axis, 0, 0, tiled=True, axis_index_groups=groups).reshape(rows.shape)


def sum_over_item(rows, n_item):
    n_far = n_item // NEAR
    near = [[far * NEAR + i for i in range(NEAR)] for far in range(n_far)]
    distant = [[far * NEAR + i for far in range(n_far)] for i in range(NEAR)]
    rows = exchange(rows, NEAR, "item", near)
    rows = exchange(add_and_copy(rows, NEAR, n_far, "add_near"), n_far, "item", distant)
    return exchange(add_and_copy(rows, n_far, NEAR, "add_far"), NEAR, "item", near)


def sum_over_stu(rows, n_stu):
    rows = exchange(rows, n_stu, "stu")
    return exchange(add_and_copy(rows, n_stu, n_stu, "add_stu"), n_stu, "stu")


def local(n_stu, n_item, attempts, item_factor, core_factor, student_weights, blocks):
    items, rank = item_factor.shape
    sums = project(attempts, item_factor.T, 2)
    raw = sum_over_item(sums.reshape(-1, BLOCK), n_item).reshape(sums.shape)
    used = items // BLOCK * rank + rank // 2
    parts, student_part = solve(raw, core_factor, student_weights, blocks, attempts, -(-used // n_stu) * n_stu)
    item_total, shared_total = finish(sum_over_stu(parts, n_stu), rank, items)
    return (item_total.T, shared_total, student_part)


def solution(mesh):
    in_specs = (P("stu", "item"), P("item", None), P(), P("stu", None), P("stu", None))
    out_specs = (P("item", None), P(), P("stu", None))
    body = functools.partial(local, mesh.shape["stu"], mesh.shape["item"])
    return jax.shard_map(body, mesh=mesh, in_specs=in_specs, out_specs=out_specs, check_vma=False)
```

```python
import functools

import jax
import jax.numpy as jnp
from jax import lax
from jax.experimental import pallas as pl
from jax.experimental.pallas import tpu as pltpu
from jax.sharding import PartitionSpec as P

NS_STEPS = 6
PROJECT_VMEM = 56 * 1024 * 1024
BLOCK = 128
NEAR = 4
RING = (0, 1, 3, 2)
F32 = jnp.float32
BF16 = jnp.bfloat16
NN = (((1,), (0,)), ((), ()))
NT = (((1,), (1,)), ((), ()))
VMEM = pl.BlockSpec(memory_space=pltpu.VMEM)
SMEM = pl.BlockSpec(memory_space=pltpu.SMEM)


def project_kernel(factor_ref, rows_ref, out_ref, factor, held, arrived, factor_arrived):
    chunks = arrived.shape[0]
    rows = held.shape[0] // chunks
    factor_load = pltpu.make_async_copy(factor_ref, factor, factor_arrived)
    factor_load.start()
    loads = []
    for chunk in range(chunks):
        place = pl.ds(chunk * rows, rows)
        loads.append(pltpu.make_async_copy(rows_ref.at[place], held.at[place], arrived.at[chunk]))
        loads[-1].start()
    factor_load.wait()
    pieces = rows // BLOCK
    for chunk in range(chunks):
        loads[chunk].wait()
        here = held[chunk * rows : (chunk + 1) * rows, :]
        product = lax.dot_general(factor[...], here, NT, preferred_element_type=F32)
        for piece in range(pieces):
            out_ref[chunk * pieces + piece] = product[:, piece * BLOCK : (piece + 1) * BLOCK]


def project(attempts, factor_t, chunks):
    row_total, items = attempts.shape
    rank = factor_t.shape[0]
    return pl.pallas_call(
        project_kernel,
        in_specs=[pl.BlockSpec(memory_space=pl.ANY)] * 2,
        out_specs=VMEM,
        out_shape=pltpu.VMEM((row_total // BLOCK, rank, BLOCK), F32),
        scratch_shapes=[
            pltpu.VMEM(factor_t.shape, BF16),
            pltpu.VMEM(attempts.shape, BF16),
            pltpu.SemaphoreType.DMA((chunks,)),
            pltpu.SemaphoreType.DMA,
        ],
        compiler_params=pltpu.CompilerParams(vmem_limit_bytes=PROJECT_VMEM),
        name="project",
    )(factor_t, attempts)


def add_kernel(in_ref, out_ref, *, parts, copies):
    rows = in_ref.shape[0] // parts
    total = in_ref[:rows, :]
    for part in range(1, parts):
        total = total + in_ref[part * rows : (part + 1) * rows, :]
    for copy in range(copies):
        out_ref[copy * rows : (copy + 1) * rows, :] = total


def add_and_copy(rows, parts, copies, name):
    out_shape = (rows.shape[0] // parts * copies, BLOCK)
    return pl.pallas_call(
        functools.partial(add_kernel, parts=parts, copies=copies),
        in_specs=[VMEM],
        out_specs=VMEM,
        out_shape=jax.ShapeDtypeStruct(out_shape, F32),
        compiler_params=pltpu.CompilerParams(vmem_limit_bytes=2 * rows.size * 4 + 1024 * 1024),
        name=name,
    )(rows)


def split(value):
    high = value.astype(BF16)
    return high, (value - high.astype(F32)).astype(BF16)


def right_factor(pair, left_lanes, right_lanes):
    parts = [half * lanes for half in split(pair) for lanes in (left_lanes, right_lanes)]
    return jnp.concatenate(parts, axis=0)


def times(left, right):
    rows = left.shape[0]
    both = jnp.concatenate([jnp.concatenate([half, half], axis=1) for half in split(left)], axis=0)
    product = jnp.dot(both, right, preferred_element_type=F32)
    return product[:rows] + product[rows:]


def solve_kernel(
    raw_ref, core_ref, weights_ref, counts_ref, attempts_ref,
    parts_ref, student_ref, halves, grams, lifts,
):
    count, rank, _ = raw_ref.shape
    students = weights_ref.shape[0]
    wide = students * rank

    ends = [counts_ref[0, 0]]
    for student in range(1, students - 1):
        ends.append(ends[-1] + counts_ref[0, student])
    owners = [sum((block >= end).astype(jnp.int32) for end in ends) for block in range(count)]
    grams[...] = jnp.zeros(grams.shape, F32)
    for block in range(count):
        both = jnp.concatenate(split(raw_ref[block]), axis=0)
        halves[block] = both
        grams[owners[block]] += lax.dot_general(both, both, NT, preferred_element_type=F32)

    lane = lax.broadcasted_iota(jnp.int32, (rank, 2 * rank), 1)
    identity = (lax.broadcasted_iota(jnp.int32, (rank, 2 * rank), 0) == lane % rank).astype(F32)
    on_left = lane[:1] < rank
    left_lanes = (lane < rank).astype(F32).astype(BF16)
    right_lanes = (lane >= rank).astype(F32).astype(BF16)

    def right(pair):
        return right_factor(pair, left_lanes, right_lanes)

    def beside(parts):
        return jnp.concatenate(parts, axis=1)

    core = core_ref[...]
    pairs = range(students // 2)
    scaled = [core * weights_ref[student : student + 1, :] for student in range(students)]
    lift = [beside(scaled[2 * pair : 2 * pair + 2]) for pair in pairs]
    lift_t = [beside([one.T for one in scaled[2 * pair : 2 * pair + 2]]) for pair in pairs]
    lift_right = [right(one) for one in lift]
    lift_t_right = [right(one) for one in lift_t]

    raw_grams = []
    for student in range(students):
        terms = grams[student]
        rows = terms[:rank] + terms[rank:]
        raw_grams.append(rows[:, :rank] + rows[:, rank:])
    raw_right = [right(beside(raw_grams[2 * pair : 2 * pair + 2])) for pair in pairs]
    gram, polynomial = [], []
    for pair in pairs:
        half_way = times(lift[pair], raw_right[pair])
        row = jnp.sum(half_way * lift[pair], axis=0, keepdims=True)
        left_trace = jnp.sum(jnp.where(on_left, row, 0.0), axis=1, keepdims=True)
        right_trace = jnp.sum(jnp.where(on_left, 0.0, row), axis=1, keepdims=True)
        inverse = 1.0 / jnp.sqrt(jnp.where(on_left, left_trace, right_trace) + 1e-06)
        gram.append(times(half_way, lift_t_right[pair]) * (inverse * inverse))
        polynomial.append(lift_t[pair] * inverse)
    for iteration in range(NS_STEPS):
        factor = [right(1.5 * identity - 0.5 * gram[pair]) for pair in pairs]
        if iteration < NS_STEPS - 1:
            moved = [times(gram[pair], factor[pair]) for pair in pairs]
            gram = [times(moved[pair], factor[pair]) for pair in pairs]
        polynomial = [times(polynomial[pair], factor[pair]) for pair in pairs]

    apply = beside([times(polynomial[pair], lift_right[pair]) for pair in pairs])
    polynomial = beside(polynomial)
    for student in range(students):
        high, low = split(apply[:, student * rank : (student + 1) * rank])
        lifts[student] = jnp.concatenate([beside([high, high]), beside([low, low])], axis=0)
    weighted = []
    for block in range(count):
        terms = jnp.dot(lifts[owners[block]], halves[block], preferred_element_type=F32)
        weighted.append((terms[:rank] + terms[rank:]).astype(BF16))
    item_part = jnp.dot(beside(weighted), attempts_ref[...], preferred_element_type=F32)

    turned = beside([polynomial[:, k * rank : (k + 1) * rank].T for k in range(students)])
    crossed = beside([times(turned[:, 2 * pair * rank : 2 * (pair + 1) * rank], raw_right[pair]) for pair in pairs])
    shared = jnp.zeros((rank, rank), F32)
    for student in range(students):
        one = crossed[:, student * rank : (student + 1) * rank]
        shared = shared + one * weights_ref[student : student + 1, :]
        student_ref[student : student + 1, :] = jnp.sum(one * core, axis=0, keepdims=True)

    tiles = item_part.shape[1] // BLOCK
    for tile in range(tiles):
        parts_ref[tile * rank : (tile + 1) * rank, :] = item_part[:, tile * BLOCK : (tile + 1) * BLOCK]
    last = tiles * rank
    parts_ref[last : last + rank // 2, :] = beside([shared[: rank // 2], shared[rank // 2 :]])


def solve(raw, core_factor, student_weights, blocks, attempts, part_rows):
    count, rank, _ = raw.shape
    students = student_weights.shape[0]
    return pl.pallas_call(
        solve_kernel,
        in_specs=[VMEM, VMEM, VMEM, SMEM, VMEM],
        out_specs=[VMEM, VMEM],
        out_shape=[
            jax.ShapeDtypeStruct((part_rows, BLOCK), F32),
            jax.ShapeDtypeStruct((students, rank), F32),
        ],
        scratch_shapes=[
            pltpu.VMEM((count, 2 * rank, BLOCK), BF16),
            pltpu.VMEM((students, 2 * rank, 2 * rank), F32),
            pltpu.VMEM((students, 2 * rank, 2 * rank), BF16),
        ],
        compiler_params=pltpu.CompilerParams(vmem_limit_bytes=16 * 1024 * 1024),
        name="solve",
    )(raw, core_factor, student_weights, blocks, attempts)


def finish_kernel(total_ref, item_ref, shared_ref):
    rank, items = item_ref.shape
    for tile in range(items // BLOCK):
        item_ref[:, tile * BLOCK : (tile + 1) * BLOCK] = total_ref[tile * rank : (tile + 1) * rank, :]
    last = items // BLOCK * rank
    both = total_ref[last : last + rank // 2, :]
    shared_ref[: rank // 2, :] = both[:, :rank]
    shared_ref[rank // 2 :, :] = both[:, rank:]


def finish(total, rank, items):
    return pl.pallas_call(
        finish_kernel,
        in_specs=[VMEM],
        out_specs=[VMEM, VMEM],
        out_shape=[
            jax.ShapeDtypeStruct((rank, items), F32),
            jax.ShapeDtypeStruct((rank, rank), F32),
        ],
        compiler_params=pltpu.CompilerParams(vmem_limit_bytes=2 * 1024 * 1024),
        name="finish",
    )(total)


def exchange(rows, parts, axis, groups=None):
    parted = rows.reshape(parts, -1, 1, BLOCK)
    return lax.all_to_all(parted, axis, 0, 0, tiled=True, axis_index_groups=groups).reshape(rows.shape)


def sum_over_item(rows):
    n_far = len(RING)
    near = [[far * NEAR + i for i in RING] for far in range(n_far)]
    distant = [[far * NEAR + i for far in RING] for i in range(NEAR)]
    rows = exchange(rows, NEAR, "item", near)
    rows = exchange(add_and_copy(rows, NEAR, n_far, "add_near"), n_far, "item", distant)
    return exchange(add_and_copy(rows, n_far, NEAR, "add_far"), NEAR, "item", near)


def sum_over_stu(rows, n_stu):
    rows = exchange(rows, n_stu, "stu")
    return exchange(add_and_copy(rows, n_stu, n_stu, "add_stu"), n_stu, "stu")


def local(n_stu, attempts, item_factor, core_factor, student_weights, blocks):
    items, rank = item_factor.shape
    sums = project(attempts, item_factor.T, 2)
    raw = sum_over_item(sums.reshape(-1, BLOCK)).reshape(sums.shape)
    used = items // BLOCK * rank + rank // 2
    parts, student_part = solve(raw, core_factor, student_weights, blocks, attempts, -(-used // n_stu) * n_stu)
    item_total, shared_total = finish(sum_over_stu(parts, n_stu), rank, items)
    return (item_total.T, shared_total, student_part)


def solution(mesh):
    in_specs = (P("stu", "item"), P("item", None), P(), P("stu", None), P("stu", None))
    out_specs = (P("item", None), P(), P("stu", None))
    body = functools.partial(local, mesh.shape["stu"])
    return jax.shard_map(body, mesh=mesh, in_specs=in_specs, out_specs=out_specs, check_vma=False)
```

```python
import functools

import jax
import jax.numpy as jnp
from jax import lax
from jax.experimental import pallas as pl
from jax.experimental.pallas import tpu as pltpu
from jax.sharding import PartitionSpec as P

NS_STEPS = 6
PROJECT_VMEM = 56 * 1024 * 1024
BLOCK = 128
NEAR_ITEM = 4
NEAR_STU = 8
RING = (0, 1, 3, 2)
F32 = jnp.float32
BF16 = jnp.bfloat16
NN = (((1,), (0,)), ((), ()))
NT = (((1,), (1,)), ((), ()))
VMEM = pl.BlockSpec(memory_space=pltpu.VMEM)
SMEM = pl.BlockSpec(memory_space=pltpu.SMEM)


def project_kernel(factor_ref, rows_ref, out_ref, factor, held, arrived, factor_arrived):
    chunks = arrived.shape[0]
    rows = held.shape[0] // chunks
    factor_load = pltpu.make_async_copy(factor_ref, factor, factor_arrived)
    factor_load.start()
    loads = []
    for chunk in range(chunks):
        place = pl.ds(chunk * rows, rows)
        loads.append(pltpu.make_async_copy(rows_ref.at[place], held.at[place], arrived.at[chunk]))
        loads[-1].start()
    factor_load.wait()
    pieces = rows // BLOCK
    for chunk in range(chunks):
        loads[chunk].wait()
        here = held[chunk * rows : (chunk + 1) * rows, :]
        product = lax.dot_general(factor[...], here, NT, preferred_element_type=F32)
        for piece in range(pieces):
            out_ref[chunk * pieces + piece] = product[:, piece * BLOCK : (piece + 1) * BLOCK]


def project(attempts, factor_t, chunks):
    row_total, items = attempts.shape
    rank = factor_t.shape[0]
    return pl.pallas_call(
        project_kernel,
        in_specs=[pl.BlockSpec(memory_space=pl.ANY)] * 2,
        out_specs=VMEM,
        out_shape=pltpu.VMEM((row_total // BLOCK, rank, BLOCK), F32),
        scratch_shapes=[
            pltpu.VMEM(factor_t.shape, BF16),
            pltpu.VMEM(attempts.shape, BF16),
            pltpu.SemaphoreType.DMA((chunks,)),
            pltpu.SemaphoreType.DMA,
        ],
        compiler_params=pltpu.CompilerParams(vmem_limit_bytes=PROJECT_VMEM),
        name="project",
    )(factor_t, attempts)


def add_kernel(in_ref, out_ref, *, parts, copies):
    rows = in_ref.shape[0] // parts
    total = in_ref[:rows, :]
    for part in range(1, parts):
        total = total + in_ref[part * rows : (part + 1) * rows, :]
    for copy in range(copies):
        out_ref[copy * rows : (copy + 1) * rows, :] = total


def add_and_copy(rows, parts, copies, name):
    out_shape = (rows.shape[0] // parts * copies, BLOCK)
    return pl.pallas_call(
        functools.partial(add_kernel, parts=parts, copies=copies),
        in_specs=[VMEM],
        out_specs=VMEM,
        out_shape=jax.ShapeDtypeStruct(out_shape, F32),
        compiler_params=pltpu.CompilerParams(vmem_limit_bytes=2 * rows.size * 4 + 1024 * 1024),
        name=name,
    )(rows)


def split(value):
    high = value.astype(BF16)
    return high, (value - high.astype(F32)).astype(BF16)


def right_factor(pair, left_lanes, right_lanes):
    parts = [half * lanes for half in split(pair) for lanes in (left_lanes, right_lanes)]
    return jnp.concatenate(parts, axis=0)


def times(left, right):
    rows = left.shape[0]
    both = jnp.concatenate([jnp.concatenate([half, half], axis=1) for half in split(left)], axis=0)
    product = jnp.dot(both, right, preferred_element_type=F32)
    return product[:rows] + product[rows:]


def solve_kernel(
    raw_ref, core_ref, weights_ref, counts_ref, attempts_ref,
    parts_ref, student_ref, halves, grams, lifts,
):
    count, rank, _ = raw_ref.shape
    students = weights_ref.shape[0]
    wide = students * rank

    ends = [counts_ref[0, 0]]
    for student in range(1, students - 1):
        ends.append(ends[-1] + counts_ref[0, student])
    owners = [sum((block >= end).astype(jnp.int32) for end in ends) for block in range(count)]
    grams[...] = jnp.zeros(grams.shape, F32)
    for block in range(count):
        both = jnp.concatenate(split(raw_ref[block]), axis=0)
        halves[block] = both
        grams[owners[block]] += lax.dot_general(both, both, NT, preferred_element_type=F32)

    lane = lax.broadcasted_iota(jnp.int32, (rank, 2 * rank), 1)
    identity = (lax.broadcasted_iota(jnp.int32, (rank, 2 * rank), 0) == lane % rank).astype(F32)
    on_left = lane[:1] < rank
    left_lanes = (lane < rank).astype(F32).astype(BF16)
    right_lanes = (lane >= rank).astype(F32).astype(BF16)

    def right(pair):
        return right_factor(pair, left_lanes, right_lanes)

    def beside(parts):
        return jnp.concatenate(parts, axis=1)

    core = core_ref[...]
    pairs = range(students // 2)
    scaled = [core * weights_ref[student : student + 1, :] for student in range(students)]
    lift = [beside(scaled[2 * pair : 2 * pair + 2]) for pair in pairs]
    lift_t = [beside([one.T for one in scaled[2 * pair : 2 * pair + 2]]) for pair in pairs]
    lift_right = [right(one) for one in lift]
    lift_t_right = [right(one) for one in lift_t]

    raw_grams = []
    for student in range(students):
        terms = grams[student]
        rows = terms[:rank] + terms[rank:]
        raw_grams.append(rows[:, :rank] + rows[:, rank:])
    raw_right = [right(beside(raw_grams[2 * pair : 2 * pair + 2])) for pair in pairs]
    gram, polynomial = [], []
    for pair in pairs:
        half_way = times(lift[pair], raw_right[pair])
        row = jnp.sum(half_way * lift[pair], axis=0, keepdims=True)
        left_trace = jnp.sum(jnp.where(on_left, row, 0.0), axis=1, keepdims=True)
        right_trace = jnp.sum(jnp.where(on_left, 0.0, row), axis=1, keepdims=True)
        inverse = 1.0 / jnp.sqrt(jnp.where(on_left, left_trace, right_trace) + 1e-06)
        gram.append(times(half_way, lift_t_right[pair]) * (inverse * inverse))
        polynomial.append(lift_t[pair] * inverse)
    for iteration in range(NS_STEPS):
        factor = [right(1.5 * identity - 0.5 * gram[pair]) for pair in pairs]
        if iteration < NS_STEPS - 1:
            moved = [times(gram[pair], factor[pair]) for pair in pairs]
            gram = [times(moved[pair], factor[pair]) for pair in pairs]
        polynomial = [times(polynomial[pair], factor[pair]) for pair in pairs]

    apply = beside([times(polynomial[pair], lift_right[pair]) for pair in pairs])
    polynomial = beside(polynomial)
    for student in range(students):
        high, low = split(apply[:, student * rank : (student + 1) * rank])
        lifts[student] = jnp.concatenate([beside([high, high]), beside([low, low])], axis=0)
    weighted = []
    for block in range(count):
        terms = jnp.dot(lifts[owners[block]], halves[block], preferred_element_type=F32)
        weighted.append((terms[:rank] + terms[rank:]).astype(BF16))
    item_part = jnp.dot(beside(weighted), attempts_ref[...], preferred_element_type=F32)

    turned = beside([polynomial[:, k * rank : (k + 1) * rank].T for k in range(students)])
    crossed = beside([times(turned[:, 2 * pair * rank : 2 * (pair + 1) * rank], raw_right[pair]) for pair in pairs])
    shared = jnp.zeros((rank, rank), F32)
    for student in range(students):
        one = crossed[:, student * rank : (student + 1) * rank]
        shared = shared + one * weights_ref[student : student + 1, :]
        student_ref[student : student + 1, :] = jnp.sum(one * core, axis=0, keepdims=True)

    tiles = item_part.shape[1] // BLOCK
    for tile in range(tiles):
        parts_ref[tile * rank : (tile + 1) * rank, :] = item_part[:, tile * BLOCK : (tile + 1) * BLOCK]
    last = tiles * rank
    parts_ref[last : last + rank // 2, :] = beside([shared[: rank // 2], shared[rank // 2 :]])


def solve(raw, core_factor, student_weights, blocks, attempts, part_rows):
    count, rank, _ = raw.shape
    students = student_weights.shape[0]
    return pl.pallas_call(
        solve_kernel,
        in_specs=[VMEM, VMEM, VMEM, SMEM, VMEM],
        out_specs=[VMEM, VMEM],
        out_shape=[
            jax.ShapeDtypeStruct((part_rows, BLOCK), F32),
            jax.ShapeDtypeStruct((students, rank), F32),
        ],
        scratch_shapes=[
            pltpu.VMEM((count, 2 * rank, BLOCK), BF16),
            pltpu.VMEM((students, 2 * rank, 2 * rank), F32),
            pltpu.VMEM((students, 2 * rank, 2 * rank), BF16),
        ],
        compiler_params=pltpu.CompilerParams(vmem_limit_bytes=16 * 1024 * 1024),
        name="solve",
    )(raw, core_factor, student_weights, blocks, attempts)


def finish_kernel(total_ref, item_ref, shared_ref):
    rank, items = item_ref.shape
    for tile in range(items // BLOCK):
        item_ref[:, tile * BLOCK : (tile + 1) * BLOCK] = total_ref[tile * rank : (tile + 1) * rank, :]
    last = items // BLOCK * rank
    both = total_ref[last : last + rank // 2, :]
    shared_ref[: rank // 2, :] = both[:, :rank]
    shared_ref[rank // 2 :, :] = both[:, rank:]


def finish(total, rank, items):
    return pl.pallas_call(
        finish_kernel,
        in_specs=[VMEM],
        out_specs=[VMEM, VMEM],
        out_shape=[
            jax.ShapeDtypeStruct((rank, items), F32),
            jax.ShapeDtypeStruct((rank, rank), F32),
        ],
        compiler_params=pltpu.CompilerParams(vmem_limit_bytes=2 * 1024 * 1024),
        name="finish",
    )(total)


def exchange(rows, parts, axis, groups=None):
    parted = rows.reshape(parts, -1, 1, BLOCK)
    return lax.all_to_all(parted, axis, 0, 0, tiled=True, axis_index_groups=groups).reshape(rows.shape)


def sum_over(axis, n_near, rows):
    n_far = len(RING)
    near = [[far * n_near + i for i in range(n_near)] for far in range(n_far)]
    distant = [[far * n_near + i for far in RING] for i in range(n_near)]
    rows = exchange(rows, n_near, axis, near)
    rows = exchange(add_and_copy(rows, n_near, n_far, "add_near_" + axis), n_far, axis, distant)
    return exchange(add_and_copy(rows, n_far, n_near, "add_far_" + axis), n_near, axis, near)


def local(n_stu, attempts, item_factor, core_factor, student_weights, blocks):
    items, rank = item_factor.shape
    sums = project(attempts, item_factor.T, 2)
    raw = sum_over("item", NEAR_ITEM, sums.reshape(-1, BLOCK)).reshape(sums.shape)
    used = items // BLOCK * rank + rank // 2
    parts, student_part = solve(raw, core_factor, student_weights, blocks, attempts, -(-used // n_stu) * n_stu)
    item_total, shared_total = finish(sum_over("stu", NEAR_STU, parts), rank, items)
    return (item_total.T, shared_total, student_part)


def solution(mesh):
    in_specs = (P("stu", "item"), P("item", None), P(), P("stu", None), P("stu", None))
    out_specs = (P("item", None), P(), P("stu", None))
    body = functools.partial(local, mesh.shape["stu"])
    return jax.shard_map(body, mesh=mesh, in_specs=in_specs, out_specs=out_specs, check_vma=False)
```

```python
import functools
import math

import jax
import jax.numpy as jnp
from jax import lax
from jax.experimental import pallas as pl
from jax.experimental.pallas import tpu as pltpu
from jax.sharding import PartitionSpec as P

NS_STEPS = 6
PROJECT_VMEM = 56 * 1024 * 1024
BLOCK = 128
NEAR_ITEM = 4
NEAR_STU = 8
RING = (0, 1, 2, 3)
F32 = jnp.float32
BF16 = jnp.bfloat16
NN = (((1,), (0,)), ((), ()))
NT = (((1,), (1,)), ((), ()))
VMEM = pl.BlockSpec(memory_space=pltpu.VMEM)
SMEM = pl.BlockSpec(memory_space=pltpu.SMEM)


def project_kernel(factor_ref, rows_ref, out_ref, factor, held, arrived, factor_arrived):
    chunks = arrived.shape[0]
    rows = held.shape[0] // chunks
    factor_load = pltpu.make_async_copy(factor_ref, factor, factor_arrived)
    factor_load.start()
    loads = []
    for chunk in range(chunks):
        place = pl.ds(chunk * rows, rows)
        loads.append(pltpu.make_async_copy(rows_ref.at[place], held.at[place], arrived.at[chunk]))
        loads[-1].start()
    factor_load.wait()
    pieces = rows // BLOCK
    for chunk in range(chunks):
        loads[chunk].wait()
        here = held[chunk * rows : (chunk + 1) * rows, :]
        product = lax.dot_general(factor[...], here, NT, preferred_element_type=F32)
        for piece in range(pieces):
            out_ref[chunk * pieces + piece] = product[:, piece * BLOCK : (piece + 1) * BLOCK]


def project(attempts, factor_t, chunks):
    row_total, items = attempts.shape
    rank = factor_t.shape[0]
    return pl.pallas_call(
        project_kernel,
        in_specs=[pl.BlockSpec(memory_space=pl.ANY)] * 2,
        out_specs=VMEM,
        out_shape=pltpu.VMEM((row_total // BLOCK, rank, BLOCK), F32),
        scratch_shapes=[
            pltpu.VMEM(factor_t.shape, BF16),
            pltpu.VMEM(attempts.shape, BF16),
            pltpu.SemaphoreType.DMA((chunks,)),
            pltpu.SemaphoreType.DMA,
        ],
        compiler_params=pltpu.CompilerParams(vmem_limit_bytes=PROJECT_VMEM),
        name="project",
    )(factor_t, attempts)


def add_kernel(in_ref, out_ref, *, parts, copies):
    rows = in_ref.shape[0] // parts
    total = in_ref[:rows, :]
    for part in range(1, parts):
        total = total + in_ref[part * rows : (part + 1) * rows, :]
    for copy in range(copies):
        out_ref[copy * rows : (copy + 1) * rows, :] = total


def add_and_copy(rows, parts, copies, name):
    out_shape = (rows.shape[0] // parts * copies, BLOCK)
    return pl.pallas_call(
        functools.partial(add_kernel, parts=parts, copies=copies),
        in_specs=[VMEM],
        out_specs=VMEM,
        out_shape=jax.ShapeDtypeStruct(out_shape, F32),
        compiler_params=pltpu.CompilerParams(vmem_limit_bytes=max(rows.size, math.prod(out_shape)) * 8 + 1024 * 1024),
        name=name,
    )(rows)


def split(value):
    high = value.astype(BF16)
    return high, (value - high.astype(F32)).astype(BF16)


def right_factor(pair, left_lanes, right_lanes):
    parts = [half * lanes for half in split(pair) for lanes in (left_lanes, right_lanes)]
    return jnp.concatenate(parts, axis=0)


def times(left, right):
    rows = left.shape[0]
    both = jnp.concatenate([jnp.concatenate([half, half], axis=1) for half in split(left)], axis=0)
    product = jnp.dot(both, right, preferred_element_type=F32)
    return product[:rows] + product[rows:]


def solve_kernel(
    raw_ref, core_ref, weights_ref, counts_ref, attempts_ref,
    parts_ref, student_ref, halves, grams, lifts,
):
    count, rank, _ = raw_ref.shape
    students = weights_ref.shape[0]
    wide = students * rank

    ends = [counts_ref[0, 0]]
    for student in range(1, students - 1):
        ends.append(ends[-1] + counts_ref[0, student])
    owners = [sum((block >= end).astype(jnp.int32) for end in ends) for block in range(count)]
    grams[...] = jnp.zeros(grams.shape, F32)
    for block in range(count):
        both = jnp.concatenate(split(raw_ref[block]), axis=0)
        halves[block] = both
        grams[owners[block]] += lax.dot_general(both, both, NT, preferred_element_type=F32)

    lane = lax.broadcasted_iota(jnp.int32, (rank, 2 * rank), 1)
    identity = (lax.broadcasted_iota(jnp.int32, (rank, 2 * rank), 0) == lane % rank).astype(F32)
    on_left = lane[:1] < rank
    left_lanes = (lane < rank).astype(F32).astype(BF16)
    right_lanes = (lane >= rank).astype(F32).astype(BF16)

    def right(pair):
        return right_factor(pair, left_lanes, right_lanes)

    def beside(parts):
        return jnp.concatenate(parts, axis=1)

    core = core_ref[...]
    pairs = range(students // 2)
    scaled = [core * weights_ref[student : student + 1, :] for student in range(students)]
    lift = [beside(scaled[2 * pair : 2 * pair + 2]) for pair in pairs]
    lift_t = [beside([one.T for one in scaled[2 * pair : 2 * pair + 2]]) for pair in pairs]
    lift_right = [right(one) for one in lift]
    lift_t_right = [right(one) for one in lift_t]

    raw_grams = []
    for student in range(students):
        terms = grams[student]
        rows = terms[:rank] + terms[rank:]
        raw_grams.append(rows[:, :rank] + rows[:, rank:])
    raw_right = [right(beside(raw_grams[2 * pair : 2 * pair + 2])) for pair in pairs]
    gram, polynomial = [], []
    for pair in pairs:
        half_way = times(lift[pair], raw_right[pair])
        row = jnp.sum(half_way * lift[pair], axis=0, keepdims=True)
        left_trace = jnp.sum(jnp.where(on_left, row, 0.0), axis=1, keepdims=True)
        right_trace = jnp.sum(jnp.where(on_left, 0.0, row), axis=1, keepdims=True)
        inverse = 1.0 / jnp.sqrt(jnp.where(on_left, left_trace, right_trace) + 1e-06)
        gram.append(times(half_way, lift_t_right[pair]) * (inverse * inverse))
        polynomial.append(lift_t[pair] * inverse)
    for iteration in range(NS_STEPS):
        factor = [right(1.5 * identity - 0.5 * gram[pair]) for pair in pairs]
        if iteration < NS_STEPS - 1:
            moved = [times(gram[pair], factor[pair]) for pair in pairs]
            gram = [times(moved[pair], factor[pair]) for pair in pairs]
        polynomial = [times(polynomial[pair], factor[pair]) for pair in pairs]

    apply = beside([times(polynomial[pair], lift_right[pair]) for pair in pairs])
    polynomial = beside(polynomial)
    for student in range(students):
        high, low = split(apply[:, student * rank : (student + 1) * rank])
        lifts[student] = jnp.concatenate([beside([high, high]), beside([low, low])], axis=0)
    weighted = []
    for block in range(count):
        terms = jnp.dot(lifts[owners[block]], halves[block], preferred_element_type=F32)
        weighted.append((terms[:rank] + terms[rank:]).astype(BF16))
    item_part = jnp.dot(beside(weighted), attempts_ref[...], preferred_element_type=F32)

    turned = beside([polynomial[:, k * rank : (k + 1) * rank].T for k in range(students)])
    crossed = beside([times(turned[:, 2 * pair * rank : 2 * (pair + 1) * rank], raw_right[pair]) for pair in pairs])
    shared = jnp.zeros((rank, rank), F32)
    for student in range(students):
        one = crossed[:, student * rank : (student + 1) * rank]
        shared = shared + one * weights_ref[student : student + 1, :]
        student_ref[student : student + 1, :] = jnp.sum(one * core, axis=0, keepdims=True)

    tiles = item_part.shape[1] // BLOCK
    for tile in range(tiles):
        parts_ref[tile * rank : (tile + 1) * rank, :] = item_part[:, tile * BLOCK : (tile + 1) * BLOCK]
    last = tiles * rank
    parts_ref[last : last + rank // 2, :] = beside([shared[: rank // 2], shared[rank // 2 :]])


def solve(raw, core_factor, student_weights, blocks, attempts, part_rows):
    count, rank, _ = raw.shape
    students = student_weights.shape[0]
    return pl.pallas_call(
        solve_kernel,
        in_specs=[VMEM, VMEM, VMEM, SMEM, VMEM],
        out_specs=[VMEM, VMEM],
        out_shape=[
            jax.ShapeDtypeStruct((part_rows, BLOCK), F32),
            jax.ShapeDtypeStruct((students, rank), F32),
        ],
        scratch_shapes=[
            pltpu.VMEM((count, 2 * rank, BLOCK), BF16),
            pltpu.VMEM((students, 2 * rank, 2 * rank), F32),
            pltpu.VMEM((students, 2 * rank, 2 * rank), BF16),
        ],
        compiler_params=pltpu.CompilerParams(vmem_limit_bytes=16 * 1024 * 1024),
        name="solve",
    )(raw, core_factor, student_weights, blocks, attempts)


def finish_kernel(total_ref, item_ref, shared_ref):
    rank, items = item_ref.shape
    for tile in range(items // BLOCK):
        item_ref[:, tile * BLOCK : (tile + 1) * BLOCK] = total_ref[tile * rank : (tile + 1) * rank, :]
    last = items // BLOCK * rank
    both = total_ref[last : last + rank // 2, :]
    shared_ref[: rank // 2, :] = both[:, :rank]
    shared_ref[rank // 2 :, :] = both[:, rank:]


def finish(total, rank, items):
    return pl.pallas_call(
        finish_kernel,
        in_specs=[VMEM],
        out_specs=[VMEM, VMEM],
        out_shape=[
            jax.ShapeDtypeStruct((rank, items), F32),
            jax.ShapeDtypeStruct((rank, rank), F32),
        ],
        compiler_params=pltpu.CompilerParams(vmem_limit_bytes=2 * 1024 * 1024),
        name="finish",
    )(total)


def exchange(rows, parts, axis, groups=None):
    parted = rows.reshape(parts, -1, 1, BLOCK)
    return lax.all_to_all(parted, axis, 0, 0, tiled=True, axis_index_groups=groups).reshape(rows.shape)


def sum_over(axis, n_near, rows, gather):
    n_far = len(RING)
    near = [[far * n_near + i for i in range(n_near)] for far in range(n_far)]
    distant = [[far * n_near + i for far in RING] for i in range(n_near)]
    rows = exchange(rows, n_near, axis, near)
    if gather:
        share = add_and_copy(rows, n_near, 1, "add_near_" + axis)
        rows = lax.all_gather(share, axis, axis_index_groups=distant, tiled=True)
    else:
        rows = exchange(add_and_copy(rows, n_near, n_far, "add_near_" + axis), n_far, axis, distant)
    return exchange(add_and_copy(rows, n_far, n_near, "add_far_" + axis), n_near, axis, near)


def local(n_stu, attempts, item_factor, core_factor, student_weights, blocks):
    items, rank = item_factor.shape
    sums = project(attempts, item_factor.T, 2)
    raw = sum_over("item", NEAR_ITEM, sums.reshape(-1, BLOCK), True).reshape(sums.shape)
    used = items // BLOCK * rank + rank // 2
    parts, student_part = solve(raw, core_factor, student_weights, blocks, attempts, -(-used // n_stu) * n_stu)
    item_total, shared_total = finish(sum_over("stu", NEAR_STU, parts, False), rank, items)
    return (item_total.T, shared_total, student_part)


def solution(mesh):
    in_specs = (P("stu", "item"), P("item", None), P(), P("stu", None), P("stu", None))
    out_specs = (P("item", None), P(), P("stu", None))
    body = functools.partial(local, mesh.shape["stu"])
    return jax.shard_map(body, mesh=mesh, in_specs=in_specs, out_specs=out_specs, check_vma=False)
```

```python
import functools
import math

import jax
import jax.numpy as jnp
from jax import lax
from jax.experimental import pallas as pl
from jax.experimental.pallas import tpu as pltpu
from jax.sharding import PartitionSpec as P

NS_STEPS = 6
PROJECT_VMEM = 56 * 1024 * 1024
BLOCK = 128
NEAR_ITEM = (0, 1, 3, 2)
NEAR_STU = (0, 1, 2, 3, 4, 5, 6, 7)
N_FAR = 4
F32 = jnp.float32
BF16 = jnp.bfloat16
NN = (((1,), (0,)), ((), ()))
NT = (((1,), (1,)), ((), ()))
VMEM = pl.BlockSpec(memory_space=pltpu.VMEM)
SMEM = pl.BlockSpec(memory_space=pltpu.SMEM)


def project_kernel(factor_ref, rows_ref, out_ref, factor, held, arrived, factor_arrived):
    chunks = arrived.shape[0]
    rows = held.shape[0] // chunks
    factor_load = pltpu.make_async_copy(factor_ref, factor, factor_arrived)
    factor_load.start()
    loads = []
    for chunk in range(chunks):
        place = pl.ds(chunk * rows, rows)
        loads.append(pltpu.make_async_copy(rows_ref.at[place], held.at[place], arrived.at[chunk]))
        loads[-1].start()
    factor_load.wait()
    pieces = rows // BLOCK
    for chunk in range(chunks):
        loads[chunk].wait()
        here = held[chunk * rows : (chunk + 1) * rows, :]
        product = lax.dot_general(factor[...], here, NT, preferred_element_type=F32)
        for piece in range(pieces):
            out_ref[chunk * pieces + piece] = product[:, piece * BLOCK : (piece + 1) * BLOCK]


def project(attempts, factor_t, chunks):
    row_total, items = attempts.shape
    rank = factor_t.shape[0]
    return pl.pallas_call(
        project_kernel,
        in_specs=[pl.BlockSpec(memory_space=pl.ANY)] * 2,
        out_specs=VMEM,
        out_shape=pltpu.VMEM((row_total // BLOCK, rank, BLOCK), F32),
        scratch_shapes=[
            pltpu.VMEM(factor_t.shape, BF16),
            pltpu.VMEM(attempts.shape, BF16),
            pltpu.SemaphoreType.DMA((chunks,)),
            pltpu.SemaphoreType.DMA,
        ],
        compiler_params=pltpu.CompilerParams(vmem_limit_bytes=PROJECT_VMEM),
        name="project",
    )(factor_t, attempts)


def add_kernel(in_ref, out_ref, *, parts, copies):
    rows = in_ref.shape[0] // parts
    total = in_ref[:rows, :]
    for part in range(1, parts):
        total = total + in_ref[part * rows : (part + 1) * rows, :]
    for copy in range(copies):
        out_ref[copy * rows : (copy + 1) * rows, :] = total


def add_and_copy(rows, parts, copies, name):
    out_shape = (rows.shape[0] // parts * copies, BLOCK)
    return pl.pallas_call(
        functools.partial(add_kernel, parts=parts, copies=copies),
        in_specs=[VMEM],
        out_specs=VMEM,
        out_shape=jax.ShapeDtypeStruct(out_shape, F32),
        compiler_params=pltpu.CompilerParams(vmem_limit_bytes=max(rows.size, math.prod(out_shape)) * 8 + 1024 * 1024),
        name=name,
    )(rows)


def split(value):
    high = value.astype(BF16)
    return high, (value - high.astype(F32)).astype(BF16)


def right_factor(pair, left_lanes, right_lanes):
    parts = [half * lanes for half in split(pair) for lanes in (left_lanes, right_lanes)]
    return jnp.concatenate(parts, axis=0)


def times(left, right):
    rows = left.shape[0]
    both = jnp.concatenate([jnp.concatenate([half, half], axis=1) for half in split(left)], axis=0)
    product = jnp.dot(both, right, preferred_element_type=F32)
    return product[:rows] + product[rows:]


def solve_kernel(
    raw_ref, core_ref, weights_ref, counts_ref, attempts_ref,
    parts_ref, student_ref, halves, grams, lifts,
):
    count, rank, _ = raw_ref.shape
    students = weights_ref.shape[0]
    wide = students * rank

    ends = [counts_ref[0, 0]]
    for student in range(1, students - 1):
        ends.append(ends[-1] + counts_ref[0, student])
    owners = [sum((block >= end).astype(jnp.int32) for end in ends) for block in range(count)]
    grams[...] = jnp.zeros(grams.shape, F32)
    for block in range(count):
        both = jnp.concatenate(split(raw_ref[block]), axis=0)
        halves[block] = both
        grams[owners[block]] += lax.dot_general(both, both, NT, preferred_element_type=F32)

    lane = lax.broadcasted_iota(jnp.int32, (rank, 2 * rank), 1)
    identity = (lax.broadcasted_iota(jnp.int32, (rank, 2 * rank), 0) == lane % rank).astype(F32)
    on_left = lane[:1] < rank
    left_lanes = (lane < rank).astype(F32).astype(BF16)
    right_lanes = (lane >= rank).astype(F32).astype(BF16)

    def right(pair):
        return right_factor(pair, left_lanes, right_lanes)

    def beside(parts):
        return jnp.concatenate(parts, axis=1)

    core = core_ref[...]
    pairs = range(students // 2)
    scaled = [core * weights_ref[student : student + 1, :] for student in range(students)]
    lift = [beside(scaled[2 * pair : 2 * pair + 2]) for pair in pairs]
    lift_t = [beside([one.T for one in scaled[2 * pair : 2 * pair + 2]]) for pair in pairs]
    lift_right = [right(one) for one in lift]
    lift_t_right = [right(one) for one in lift_t]

    raw_grams = []
    for student in range(students):
        terms = grams[student]
        rows = terms[:rank] + terms[rank:]
        raw_grams.append(rows[:, :rank] + rows[:, rank:])
    raw_right = [right(beside(raw_grams[2 * pair : 2 * pair + 2])) for pair in pairs]
    gram, polynomial = [], []
    for pair in pairs:
        half_way = times(lift[pair], raw_right[pair])
        row = jnp.sum(half_way * lift[pair], axis=0, keepdims=True)
        left_trace = jnp.sum(jnp.where(on_left, row, 0.0), axis=1, keepdims=True)
        right_trace = jnp.sum(jnp.where(on_left, 0.0, row), axis=1, keepdims=True)
        inverse = 1.0 / jnp.sqrt(jnp.where(on_left, left_trace, right_trace) + 1e-06)
        gram.append(times(half_way, lift_t_right[pair]) * (inverse * inverse))
        polynomial.append(lift_t[pair] * inverse)
    for iteration in range(NS_STEPS):
        factor = [right(1.5 * identity - 0.5 * gram[pair]) for pair in pairs]
        if iteration < NS_STEPS - 1:
            moved = [times(gram[pair], factor[pair]) for pair in pairs]
            gram = [times(moved[pair], factor[pair]) for pair in pairs]
        polynomial = [times(polynomial[pair], factor[pair]) for pair in pairs]

    apply = beside([times(polynomial[pair], lift_right[pair]) for pair in pairs])
    polynomial = beside(polynomial)
    for student in range(students):
        high, low = split(apply[:, student * rank : (student + 1) * rank])
        lifts[student] = jnp.concatenate([beside([high, high]), beside([low, low])], axis=0)
    weighted = []
    for block in range(count):
        terms = jnp.dot(lifts[owners[block]], halves[block], preferred_element_type=F32)
        weighted.append((terms[:rank] + terms[rank:]).astype(BF16))
    item_part = jnp.dot(beside(weighted), attempts_ref[...], preferred_element_type=F32)

    turned = beside([polynomial[:, k * rank : (k + 1) * rank].T for k in range(students)])
    crossed = beside([times(turned[:, 2 * pair * rank : 2 * (pair + 1) * rank], raw_right[pair]) for pair in pairs])
    shared = jnp.zeros((rank, rank), F32)
    for student in range(students):
        one = crossed[:, student * rank : (student + 1) * rank]
        shared = shared + one * weights_ref[student : student + 1, :]
        student_ref[student : student + 1, :] = jnp.sum(one * core, axis=0, keepdims=True)

    tiles = item_part.shape[1] // BLOCK
    for tile in range(tiles):
        parts_ref[tile * rank : (tile + 1) * rank, :] = item_part[:, tile * BLOCK : (tile + 1) * BLOCK]
    last = tiles * rank
    parts_ref[last : last + rank // 2, :] = beside([shared[: rank // 2], shared[rank // 2 :]])


def solve(raw, core_factor, student_weights, blocks, attempts, part_rows):
    count, rank, _ = raw.shape
    students = student_weights.shape[0]
    return pl.pallas_call(
        solve_kernel,
        in_specs=[VMEM, VMEM, VMEM, SMEM, VMEM],
        out_specs=[VMEM, VMEM],
        out_shape=[
            jax.ShapeDtypeStruct((part_rows, BLOCK), F32),
            jax.ShapeDtypeStruct((students, rank), F32),
        ],
        scratch_shapes=[
            pltpu.VMEM((count, 2 * rank, BLOCK), BF16),
            pltpu.VMEM((students, 2 * rank, 2 * rank), F32),
            pltpu.VMEM((students, 2 * rank, 2 * rank), BF16),
        ],
        compiler_params=pltpu.CompilerParams(vmem_limit_bytes=16 * 1024 * 1024),
        name="solve",
    )(raw, core_factor, student_weights, blocks, attempts)


def finish_kernel(total_ref, item_ref, shared_ref):
    rank, items = item_ref.shape
    for tile in range(items // BLOCK):
        item_ref[:, tile * BLOCK : (tile + 1) * BLOCK] = total_ref[tile * rank : (tile + 1) * rank, :]
    last = items // BLOCK * rank
    both = total_ref[last : last + rank // 2, :]
    shared_ref[: rank // 2, :] = both[:, :rank]
    shared_ref[rank // 2 :, :] = both[:, rank:]


def finish(total, rank, items):
    return pl.pallas_call(
        finish_kernel,
        in_specs=[VMEM],
        out_specs=[VMEM, VMEM],
        out_shape=[
            jax.ShapeDtypeStruct((rank, items), F32),
            jax.ShapeDtypeStruct((rank, rank), F32),
        ],
        compiler_params=pltpu.CompilerParams(vmem_limit_bytes=2 * 1024 * 1024),
        name="finish",
    )(total)


def exchange(rows, parts, axis, groups=None):
    parted = rows.reshape(parts, -1, 1, BLOCK)
    return lax.all_to_all(parted, axis, 0, 0, tiled=True, axis_index_groups=groups).reshape(rows.shape)


def sum_over(axis, order, rows, gather):
    n_near = len(order)
    near = [[far * n_near + i for i in order] for far in range(N_FAR)]
    distant = [[far * n_near + i for far in range(N_FAR)] for i in range(n_near)]
    rows = exchange(rows, n_near, axis, near)
    if gather:
        share = add_and_copy(rows, n_near, 1, "add_near_" + axis)
        rows = lax.all_gather(share, axis, axis_index_groups=distant, tiled=True)
    else:
        rows = exchange(add_and_copy(rows, n_near, N_FAR, "add_near_" + axis), N_FAR, axis, distant)
    return exchange(add_and_copy(rows, N_FAR, n_near, "add_far_" + axis), n_near, axis, near)


def local(n_stu, attempts, item_factor, core_factor, student_weights, blocks):
    items, rank = item_factor.shape
    sums = project(attempts, item_factor.T, 2)
    raw = sum_over("item", NEAR_ITEM, sums.reshape(-1, BLOCK), True).reshape(sums.shape)
    used = items // BLOCK * rank + rank // 2
    parts, student_part = solve(raw, core_factor, student_weights, blocks, attempts, -(-used // n_stu) * n_stu)
    item_total, shared_total = finish(sum_over("stu", NEAR_STU, parts, False), rank, items)
    return (item_total.T, shared_total, student_part)


def solution(mesh):
    in_specs = (P("stu", "item"), P("item", None), P(), P("stu", None), P("stu", None))
    out_specs = (P("item", None), P(), P("stu", None))
    body = functools.partial(local, mesh.shape["stu"])
    return jax.shard_map(body, mesh=mesh, in_specs=in_specs, out_specs=out_specs, check_vma=False)
```

```python
import functools
import math

import jax
import jax.numpy as jnp
from jax import lax
from jax.experimental import pallas as pl
from jax.experimental.pallas import tpu as pltpu
from jax.sharding import PartitionSpec as P

NS_STEPS = 6
PROJECT_VMEM = 56 * 1024 * 1024
BLOCK = 128
NEAR_ITEM = (0, 1, 3, 2)
NEAR_STU = (0, 1, 2, 3, 4, 5, 6, 7)
N_FAR = 4
F32 = jnp.float32
BF16 = jnp.bfloat16
NN = (((1,), (0,)), ((), ()))
NT = (((1,), (1,)), ((), ()))
VMEM = pl.BlockSpec(memory_space=pltpu.VMEM)
SMEM = pl.BlockSpec(memory_space=pltpu.SMEM)


def project_kernel(factor_ref, rows_ref, out_ref, factor, held, arrived, factor_arrived):
    chunks = arrived.shape[0]
    rows = held.shape[0] // chunks
    factor_load = pltpu.make_async_copy(factor_ref, factor, factor_arrived)
    factor_load.start()
    loads = []
    for chunk in range(chunks):
        place = pl.ds(chunk * rows, rows)
        loads.append(pltpu.make_async_copy(rows_ref.at[place], held.at[place], arrived.at[chunk]))
        loads[-1].start()
    factor_load.wait()
    pieces = rows // BLOCK
    for chunk in range(chunks):
        loads[chunk].wait()
        here = held[chunk * rows : (chunk + 1) * rows, :]
        product = lax.dot_general(factor[...], here, NT, preferred_element_type=F32)
        for piece in range(pieces):
            out_ref[chunk * pieces + piece] = product[:, piece * BLOCK : (piece + 1) * BLOCK]


def project(attempts, factor_t, chunks):
    row_total, items = attempts.shape
    rank = factor_t.shape[0]
    return pl.pallas_call(
        project_kernel,
        in_specs=[pl.BlockSpec(memory_space=pl.ANY)] * 2,
        out_specs=VMEM,
        out_shape=pltpu.VMEM((row_total // BLOCK, rank, BLOCK), F32),
        scratch_shapes=[
            pltpu.VMEM(factor_t.shape, BF16),
            pltpu.VMEM(attempts.shape, BF16),
            pltpu.SemaphoreType.DMA((chunks,)),
            pltpu.SemaphoreType.DMA,
        ],
        compiler_params=pltpu.CompilerParams(vmem_limit_bytes=PROJECT_VMEM),
        name="project",
    )(factor_t, attempts)


def add_kernel(in_ref, out_ref, *, parts, copies):
    rows = in_ref.shape[0] // parts
    total = in_ref[:rows, :]
    for part in range(1, parts):
        total = total + in_ref[part * rows : (part + 1) * rows, :]
    for copy in range(copies):
        out_ref[copy * rows : (copy + 1) * rows, :] = total


def add_and_copy(rows, parts, copies, name):
    out_shape = (rows.shape[0] // parts * copies, BLOCK)
    return pl.pallas_call(
        functools.partial(add_kernel, parts=parts, copies=copies),
        in_specs=[VMEM],
        out_specs=VMEM,
        out_shape=jax.ShapeDtypeStruct(out_shape, F32),
        compiler_params=pltpu.CompilerParams(vmem_limit_bytes=max(rows.size, math.prod(out_shape)) * 8 + 1024 * 1024),
        name=name,
    )(rows)


def split(value):
    high = value.astype(BF16)
    return high, (value - high.astype(F32)).astype(BF16)


def right_factor(pair, left_lanes, right_lanes):
    parts = [half * lanes for half in split(pair) for lanes in (left_lanes, right_lanes)]
    return jnp.concatenate(parts, axis=0)


def times(left, right):
    rows = left.shape[0]
    both = jnp.concatenate([jnp.concatenate([half, half], axis=1) for half in split(left)], axis=0)
    product = jnp.dot(both, right, preferred_element_type=F32)
    return product[:rows] + product[rows:]


def solve_kernel(
    raw_ref, core_ref, weights_ref, counts_ref, attempts_ref,
    parts_ref, student_ref, halves, grams, lifts,
):
    count, rank, _ = raw_ref.shape
    students = weights_ref.shape[0]
    wide = students * rank

    ends = [counts_ref[0, 0]]
    for student in range(1, students - 1):
        ends.append(ends[-1] + counts_ref[0, student])
    owners = [sum((block >= end).astype(jnp.int32) for end in ends) for block in range(count)]
    grams[...] = jnp.zeros(grams.shape, F32)
    for block in range(count):
        both = jnp.concatenate(split(raw_ref[block]), axis=0)
        halves[block] = both
        grams[owners[block]] += lax.dot_general(both, both, NT, preferred_element_type=F32)

    lane = lax.broadcasted_iota(jnp.int32, (rank, 2 * rank), 1)
    identity = (lax.broadcasted_iota(jnp.int32, (rank, 2 * rank), 0) == lane % rank).astype(F32)
    on_left = lane[:1] < rank
    left_lanes = (lane < rank).astype(F32).astype(BF16)
    right_lanes = (lane >= rank).astype(F32).astype(BF16)

    def right(pair):
        return right_factor(pair, left_lanes, right_lanes)

    def beside(parts):
        return jnp.concatenate(parts, axis=1)

    core = core_ref[...]
    pairs = range(students // 2)
    scaled = [core * weights_ref[student : student + 1, :] for student in range(students)]
    lift = [beside(scaled[2 * pair : 2 * pair + 2]) for pair in pairs]
    lift_t = [beside([one.T for one in scaled[2 * pair : 2 * pair + 2]]) for pair in pairs]
    lift_right = [right(one) for one in lift]
    lift_t_right = [right(one) for one in lift_t]

    raw_grams = []
    for student in range(students):
        terms = grams[student]
        rows = terms[:rank] + terms[rank:]
        raw_grams.append(rows[:, :rank] + rows[:, rank:])
    raw_right = [right(beside(raw_grams[2 * pair : 2 * pair + 2])) for pair in pairs]
    gram, polynomial = [], []
    for pair in pairs:
        half_way = times(lift[pair], raw_right[pair])
        row = jnp.sum(half_way * lift[pair], axis=0, keepdims=True)
        left_trace = jnp.sum(jnp.where(on_left, row, 0.0), axis=1, keepdims=True)
        right_trace = jnp.sum(jnp.where(on_left, 0.0, row), axis=1, keepdims=True)
        inverse = 1.0 / jnp.sqrt(jnp.where(on_left, left_trace, right_trace) + 1e-06)
        gram.append(times(half_way, lift_t_right[pair]) * (inverse * inverse))
        polynomial.append(lift_t[pair] * inverse)
    for iteration in range(NS_STEPS - 1):
        factor = [1.5 * identity - 0.5 * gram[pair] for pair in pairs]
        factor_right = [right(factor[pair]) for pair in pairs]
        moved = [times(gram[pair], factor_right[pair]) for pair in pairs]
        if iteration < NS_STEPS - 2:
            gram = [times(moved[pair], factor_right[pair]) for pair in pairs]
        polynomial = [times(polynomial[pair], factor_right[pair]) for pair in pairs]
    ahead = [right(times(factor[pair], lift_right[pair])) for pair in pairs]
    bent = [times(polynomial[pair], right(moved[pair])) for pair in pairs]
    straight = [times(polynomial[pair], lift_right[pair]) for pair in pairs]
    apply = beside([1.5 * straight[pair] - 0.5 * times(bent[pair], ahead[pair]) for pair in pairs])
    polynomial = beside([1.5 * polynomial[pair] - 0.5 * times(bent[pair], factor_right[pair]) for pair in pairs])
    for student in range(students):
        high, low = split(apply[:, student * rank : (student + 1) * rank])
        lifts[student] = jnp.concatenate([beside([high, high]), beside([low, low])], axis=0)
    weighted = []
    for block in range(count):
        terms = jnp.dot(lifts[owners[block]], halves[block], preferred_element_type=F32)
        weighted.append((terms[:rank] + terms[rank:]).astype(BF16))
    item_part = jnp.dot(beside(weighted), attempts_ref[...], preferred_element_type=F32)

    turned = beside([polynomial[:, k * rank : (k + 1) * rank].T for k in range(students)])
    crossed = beside([times(turned[:, 2 * pair * rank : 2 * (pair + 1) * rank], raw_right[pair]) for pair in pairs])
    shared = jnp.zeros((rank, rank), F32)
    for student in range(students):
        one = crossed[:, student * rank : (student + 1) * rank]
        shared = shared + one * weights_ref[student : student + 1, :]
        student_ref[student : student + 1, :] = jnp.sum(one * core, axis=0, keepdims=True)

    tiles = item_part.shape[1] // BLOCK
    for tile in range(tiles):
        parts_ref[tile * rank : (tile + 1) * rank, :] = item_part[:, tile * BLOCK : (tile + 1) * BLOCK]
    last = tiles * rank
    parts_ref[last : last + rank // 2, :] = beside([shared[: rank // 2], shared[rank // 2 :]])


def solve(raw, core_factor, student_weights, blocks, attempts, part_rows):
    count, rank, _ = raw.shape
    students = student_weights.shape[0]
    return pl.pallas_call(
        solve_kernel,
        in_specs=[VMEM, VMEM, VMEM, SMEM, VMEM],
        out_specs=[VMEM, VMEM],
        out_shape=[
            jax.ShapeDtypeStruct((part_rows, BLOCK), F32),
            jax.ShapeDtypeStruct((students, rank), F32),
        ],
        scratch_shapes=[
            pltpu.VMEM((count, 2 * rank, BLOCK), BF16),
            pltpu.VMEM((students, 2 * rank, 2 * rank), F32),
            pltpu.VMEM((students, 2 * rank, 2 * rank), BF16),
        ],
        compiler_params=pltpu.CompilerParams(vmem_limit_bytes=16 * 1024 * 1024),
        name="solve",
    )(raw, core_factor, student_weights, blocks, attempts)


def finish_kernel(total_ref, item_ref, shared_ref):
    rank, items = item_ref.shape
    for tile in range(items // BLOCK):
        item_ref[:, tile * BLOCK : (tile + 1) * BLOCK] = total_ref[tile * rank : (tile + 1) * rank, :]
    last = items // BLOCK * rank
    both = total_ref[last : last + rank // 2, :]
    shared_ref[: rank // 2, :] = both[:, :rank]
    shared_ref[rank // 2 :, :] = both[:, rank:]


def finish(total, rank, items):
    return pl.pallas_call(
        finish_kernel,
        in_specs=[VMEM],
        out_specs=[VMEM, VMEM],
        out_shape=[
            jax.ShapeDtypeStruct((rank, items), F32),
            jax.ShapeDtypeStruct((rank, rank), F32),
        ],
        compiler_params=pltpu.CompilerParams(vmem_limit_bytes=2 * 1024 * 1024),
        name="finish",
    )(total)


def exchange(rows, parts, axis, groups=None):
    parted = rows.reshape(parts, -1, 1, BLOCK)
    return lax.all_to_all(parted, axis, 0, 0, tiled=True, axis_index_groups=groups).reshape(rows.shape)


def sum_over(axis, order, rows, gather):
    n_near = len(order)
    near = [[far * n_near + i for i in order] for far in range(N_FAR)]
    distant = [[far * n_near + i for far in range(N_FAR)] for i in range(n_near)]
    rows = exchange(rows, n_near, axis, near)
    if gather:
        share = add_and_copy(rows, n_near, 1, "add_near_" + axis)
        rows = lax.all_gather(share, axis, axis_index_groups=distant, tiled=True)
    else:
        rows = exchange(add_and_copy(rows, n_near, N_FAR, "add_near_" + axis), N_FAR, axis, distant)
    return exchange(add_and_copy(rows, N_FAR, n_near, "add_far_" + axis), n_near, axis, near)


def local(n_stu, attempts, item_factor, core_factor, student_weights, blocks):
    items, rank = item_factor.shape
    sums = project(attempts, item_factor.T, 2)
    raw = sum_over("item", NEAR_ITEM, sums.reshape(-1, BLOCK), True).reshape(sums.shape)
    used = items // BLOCK * rank + rank // 2
    parts, student_part = solve(raw, core_factor, student_weights, blocks, attempts, -(-used // n_stu) * n_stu)
    item_total, shared_total = finish(sum_over("stu", NEAR_STU, parts, False), rank, items)
    return (item_total.T, shared_total, student_part)


def solution(mesh):
    in_specs = (P("stu", "item"), P("item", None), P(), P("stu", None), P("stu", None))
    out_specs = (P("item", None), P(), P("stu", None))
    body = functools.partial(local, mesh.shape["stu"])
    return jax.shard_map(body, mesh=mesh, in_specs=in_specs, out_specs=out_specs, check_vma=False)
```

```python
import functools
import math

import jax
import jax.numpy as jnp
from jax import lax
from jax.experimental import pallas as pl
from jax.experimental.pallas import tpu as pltpu
from jax.sharding import PartitionSpec as P

NS_STEPS = 6
PROJECT_VMEM = 56 * 1024 * 1024
BLOCK = 128
NEAR_ITEM = (0, 1, 3, 2)
NEAR_STU = (0, 1, 2, 3, 4, 5, 6, 7)
N_FAR = 4
F32 = jnp.float32
BF16 = jnp.bfloat16
NN = (((1,), (0,)), ((), ()))
NT = (((1,), (1,)), ((), ()))
VMEM = pl.BlockSpec(memory_space=pltpu.VMEM)
SMEM = pl.BlockSpec(memory_space=pltpu.SMEM)


def project_kernel(factor_ref, rows_ref, out_ref, factor, held, arrived, factor_arrived):
    chunks = arrived.shape[0]
    rows = held.shape[0] // chunks
    factor_load = pltpu.make_async_copy(factor_ref, factor, factor_arrived)
    factor_load.start()
    loads = []
    for chunk in range(chunks):
        place = pl.ds(chunk * rows, rows)
        loads.append(pltpu.make_async_copy(rows_ref.at[place], held.at[place], arrived.at[chunk]))
        loads[-1].start()
    factor_load.wait()
    pieces = rows // BLOCK
    for chunk in range(chunks):
        loads[chunk].wait()
        here = held[chunk * rows : (chunk + 1) * rows, :]
        product = lax.dot_general(factor[...], here, NT, preferred_element_type=F32)
        for piece in range(pieces):
            out_ref[chunk * pieces + piece] = product[:, piece * BLOCK : (piece + 1) * BLOCK]


def project(attempts, factor_t, chunks):
    row_total, items = attempts.shape
    rank = factor_t.shape[0]
    return pl.pallas_call(
        project_kernel,
        in_specs=[pl.BlockSpec(memory_space=pl.ANY)] * 2,
        out_specs=VMEM,
        out_shape=pltpu.VMEM((row_total // BLOCK, rank, BLOCK), F32),
        scratch_shapes=[
            pltpu.VMEM(factor_t.shape, BF16),
            pltpu.VMEM(attempts.shape, BF16),
            pltpu.SemaphoreType.DMA((chunks,)),
            pltpu.SemaphoreType.DMA,
        ],
        compiler_params=pltpu.CompilerParams(vmem_limit_bytes=PROJECT_VMEM),
        name="project",
    )(factor_t, attempts)


def add_kernel(in_ref, out_ref, *, parts, copies):
    rows = in_ref.shape[0] // parts
    total = in_ref[:rows, :]
    for part in range(1, parts):
        total = total + in_ref[part * rows : (part + 1) * rows, :]
    for copy in range(copies):
        out_ref[copy * rows : (copy + 1) * rows, :] = total


def add_and_copy(rows, parts, copies, name):
    out_shape = (rows.shape[0] // parts * copies, BLOCK)
    return pl.pallas_call(
        functools.partial(add_kernel, parts=parts, copies=copies),
        in_specs=[VMEM],
        out_specs=VMEM,
        out_shape=jax.ShapeDtypeStruct(out_shape, F32),
        compiler_params=pltpu.CompilerParams(vmem_limit_bytes=max(rows.size, math.prod(out_shape)) * 8 + 1024 * 1024),
        name=name,
    )(rows)


def split(value):
    high = value.astype(BF16)
    return high, (value - high.astype(F32)).astype(BF16)


def right_factor(pair, left_lanes, right_lanes):
    parts = [half * lanes for half in split(pair) for lanes in (left_lanes, right_lanes)]
    return jnp.concatenate(parts, axis=0)


def times(left, right):
    rows = left.shape[0]
    both = jnp.concatenate([jnp.concatenate([half, half], axis=1) for half in split(left)], axis=0)
    product = jnp.dot(both, right, preferred_element_type=F32)
    return product[:rows] + product[rows:]


def solve_kernel(
    raw_ref, core_ref, weights_ref, counts_ref, attempts_ref,
    parts_ref, student_ref, halves, grams, lifts,
):
    count, rank, _ = raw_ref.shape
    students = weights_ref.shape[0]
    wide = students * rank

    ends = [counts_ref[0, 0]]
    for student in range(1, students - 1):
        ends.append(ends[-1] + counts_ref[0, student])
    owners = [sum((block >= end).astype(jnp.int32) for end in ends) for block in range(count)]
    grams[...] = jnp.zeros(grams.shape, F32)
    for block in range(count):
        both = jnp.concatenate(split(raw_ref[block]), axis=0)
        halves[block] = both
        grams[owners[block]] += lax.dot_general(both, both, NT, preferred_element_type=F32)

    lane = lax.broadcasted_iota(jnp.int32, (rank, 2 * rank), 1)
    identity = (lax.broadcasted_iota(jnp.int32, (rank, 2 * rank), 0) == lane % rank).astype(F32)
    on_left = lane[:1] < rank
    left_lanes = (lane < rank).astype(F32).astype(BF16)
    right_lanes = (lane >= rank).astype(F32).astype(BF16)

    def right(pair):
        return right_factor(pair, left_lanes, right_lanes)

    def beside(parts):
        return jnp.concatenate(parts, axis=1)

    core = core_ref[...]
    pairs = range(students // 2)
    scaled = [core * weights_ref[student : student + 1, :] for student in range(students)]
    lift = [beside(scaled[2 * pair : 2 * pair + 2]) for pair in pairs]
    lift_t = [beside([one.T for one in scaled[2 * pair : 2 * pair + 2]]) for pair in pairs]
    lift_right = [right(one) for one in lift]
    lift_t_right = [right(one) for one in lift_t]

    raw_grams = []
    for student in range(students):
        terms = grams[student]
        rows = terms[:rank] + terms[rank:]
        raw_grams.append(rows[:, :rank] + rows[:, rank:])
    raw_right = [right(beside(raw_grams[2 * pair : 2 * pair + 2])) for pair in pairs]
    gram, polynomial = [], []
    for pair in pairs:
        half_way = times(lift[pair], raw_right[pair])
        row = jnp.sum(half_way * lift[pair], axis=0, keepdims=True)
        left_trace = jnp.sum(jnp.where(on_left, row, 0.0), axis=1, keepdims=True)
        right_trace = jnp.sum(jnp.where(on_left, 0.0, row), axis=1, keepdims=True)
        inverse = 1.0 / jnp.sqrt(jnp.where(on_left, left_trace, right_trace) + 1e-06)
        gram.append(times(half_way, lift_t_right[pair]) * (inverse * inverse))
        polynomial.append(lift_t[pair] * inverse)
    for iteration in range(NS_STEPS - 1):
        factor = [1.5 * identity - 0.5 * gram[pair] for pair in pairs]
        factor_right = [right(factor[pair]) for pair in pairs]
        moved = [times(gram[pair], factor_right[pair]) for pair in pairs]
        if iteration < NS_STEPS - 2:
            gram = [times(moved[pair], factor_right[pair]) for pair in pairs]
        polynomial = [times(polynomial[pair], factor_right[pair]) for pair in pairs]
    ahead = [right(times(factor[pair], lift_right[pair])) for pair in pairs]
    bent = [times(polynomial[pair], right(moved[pair])) for pair in pairs]
    straight = [times(polynomial[pair], lift_right[pair]) for pair in pairs]
    apply = beside([1.5 * straight[pair] - 0.5 * times(bent[pair], ahead[pair]) for pair in pairs])
    polynomial = beside([1.5 * polynomial[pair] - 0.5 * times(bent[pair], factor_right[pair]) for pair in pairs])
    for student in range(students):
        high, low = split(apply[:, student * rank : (student + 1) * rank])
        lifts[student] = jnp.concatenate([beside([high, high]), beside([low, low])], axis=0)
    weighted = []
    for block in range(count):
        terms = jnp.dot(lifts[owners[block]], halves[block], preferred_element_type=F32)
        weighted.append((terms[:rank] + terms[rank:]).astype(BF16))
    item_part = jnp.dot(beside(weighted), attempts_ref[...], preferred_element_type=F32)

    turned = beside([polynomial[:, k * rank : (k + 1) * rank].T for k in range(students)])
    crossed = beside([times(turned[:, 2 * pair * rank : 2 * (pair + 1) * rank], raw_right[pair]) for pair in pairs])
    shared = jnp.zeros((rank, rank), F32)
    for student in range(students):
        one = crossed[:, student * rank : (student + 1) * rank]
        shared = shared + one * weights_ref[student : student + 1, :]
        student_ref[student : student + 1, :] = jnp.sum(one * core, axis=0, keepdims=True)

    tiles = item_part.shape[1] // BLOCK
    for tile in range(tiles):
        parts_ref[tile * rank : (tile + 1) * rank, :] = item_part[:, tile * BLOCK : (tile + 1) * BLOCK]
    last = tiles * rank
    parts_ref[last : last + rank // 2, :] = beside([shared[: rank // 2], shared[rank // 2 :]])
    used = last + rank // 2
    if parts_ref.shape[0] > used:
        parts_ref[used:, :] = jnp.zeros((parts_ref.shape[0] - used, BLOCK), F32)


def solve(raw, core_factor, student_weights, blocks, attempts, part_rows):
    count, rank, _ = raw.shape
    students = student_weights.shape[0]
    return pl.pallas_call(
        solve_kernel,
        in_specs=[VMEM, VMEM, VMEM, SMEM, VMEM],
        out_specs=[VMEM, VMEM],
        out_shape=[
            jax.ShapeDtypeStruct((part_rows, BLOCK), F32),
            jax.ShapeDtypeStruct((students, rank), F32),
        ],
        scratch_shapes=[
            pltpu.VMEM((count, 2 * rank, BLOCK), BF16),
            pltpu.VMEM((students, 2 * rank, 2 * rank), F32),
            pltpu.VMEM((students, 2 * rank, 2 * rank), BF16),
        ],
        compiler_params=pltpu.CompilerParams(vmem_limit_bytes=16 * 1024 * 1024),
        name="solve",
    )(raw, core_factor, student_weights, blocks, attempts)


def finish_kernel(total_ref, item_ref, shared_ref):
    rank, items = item_ref.shape
    for tile in range(items // BLOCK):
        item_ref[:, tile * BLOCK : (tile + 1) * BLOCK] = total_ref[tile * rank : (tile + 1) * rank, :]
    last = items // BLOCK * rank
    both = total_ref[last : last + rank // 2, :]
    shared_ref[: rank // 2, :] = both[:, :rank]
    shared_ref[rank // 2 :, :] = both[:, rank:]


def finish(total, rank, items):
    return pl.pallas_call(
        finish_kernel,
        in_specs=[VMEM],
        out_specs=[VMEM, VMEM],
        out_shape=[
            jax.ShapeDtypeStruct((rank, items), F32),
            jax.ShapeDtypeStruct((rank, rank), F32),
        ],
        compiler_params=pltpu.CompilerParams(vmem_limit_bytes=2 * 1024 * 1024),
        name="finish",
    )(total)


def exchange(rows, parts, axis, groups=None):
    parted = rows.reshape(parts, -1, 1, BLOCK)
    return lax.all_to_all(parted, axis, 0, 0, tiled=True, axis_index_groups=groups).reshape(rows.shape)


def sum_over(axis, order, rows, gather):
    n_near = len(order)
    near = [[far * n_near + i for i in order] for far in range(N_FAR)]
    distant = [[far * n_near + i for far in range(N_FAR)] for i in range(n_near)]
    rows = exchange(rows, n_near, axis, near)
    if gather:
        share = add_and_copy(rows, n_near, 1, "add_near_" + axis)
        rows = lax.all_gather(share, axis, axis_index_groups=distant, tiled=True)
    else:
        rows = exchange(add_and_copy(rows, n_near, N_FAR, "add_near_" + axis), N_FAR, axis, distant)
    return exchange(add_and_copy(rows, N_FAR, n_near, "add_far_" + axis), n_near, axis, near)


def local(attempts, item_factor, core_factor, student_weights, blocks):
    items, rank = item_factor.shape
    sums = project(attempts, item_factor.T, 2)
    raw = sum_over("item", NEAR_ITEM, sums.reshape(-1, BLOCK), True).reshape(sums.shape)
    used = items // BLOCK * rank + rank // 2
    step = 8 * len(NEAR_STU)
    parts, student_part = solve(raw, core_factor, student_weights, blocks, attempts, -(-used // step) * step)
    item_total, shared_total = finish(sum_over("stu", NEAR_STU, parts, False), rank, items)
    return (item_total.T, shared_total, student_part)


def solution(mesh):
    in_specs = (P("stu", "item"), P("item", None), P(), P("stu", None), P("stu", None))
    out_specs = (P("item", None), P(), P("stu", None))
    return jax.shard_map(local, mesh=mesh, in_specs=in_specs, out_specs=out_specs, check_vma=False)
```

```python
import functools
import math

import jax
import jax.numpy as jnp
from jax import lax
from jax.experimental import pallas as pl
from jax.experimental.pallas import tpu as pltpu
from jax.sharding import PartitionSpec as P

NS_STEPS = 6
PROJECT_VMEM = 56 * 1024 * 1024
BLOCK = 128
NEAR_ITEM = (0, 1, 3, 2)
NEAR_STU = (0, 1, 2, 3, 4, 5, 6, 7)
N_FAR = 4
RING = (0, 1, 3, 2)
F32 = jnp.float32
BF16 = jnp.bfloat16
NN = (((1,), (0,)), ((), ()))
NT = (((1,), (1,)), ((), ()))
VMEM = pl.BlockSpec(memory_space=pltpu.VMEM)
SMEM = pl.BlockSpec(memory_space=pltpu.SMEM)


def project_kernel(factor_ref, rows_ref, out_ref, factor, held, arrived, factor_arrived):
    chunks = arrived.shape[0]
    rows = held.shape[0] // chunks
    factor_load = pltpu.make_async_copy(factor_ref, factor, factor_arrived)
    factor_load.start()
    loads = []
    for chunk in range(chunks):
        place = pl.ds(chunk * rows, rows)
        loads.append(pltpu.make_async_copy(rows_ref.at[place], held.at[place], arrived.at[chunk]))
        loads[-1].start()
    factor_load.wait()
    pieces = rows // BLOCK
    for chunk in range(chunks):
        loads[chunk].wait()
        here = held[chunk * rows : (chunk + 1) * rows, :]
        product = lax.dot_general(factor[...], here, NT, preferred_element_type=F32)
        for piece in range(pieces):
            out_ref[chunk * pieces + piece] = product[:, piece * BLOCK : (piece + 1) * BLOCK]


def project(attempts, factor_t, chunks):
    row_total, items = attempts.shape
    rank = factor_t.shape[0]
    return pl.pallas_call(
        project_kernel,
        in_specs=[pl.BlockSpec(memory_space=pl.ANY)] * 2,
        out_specs=VMEM,
        out_shape=pltpu.VMEM((row_total // BLOCK, rank, BLOCK), F32),
        scratch_shapes=[
            pltpu.VMEM(factor_t.shape, BF16),
            pltpu.VMEM(attempts.shape, BF16),
            pltpu.SemaphoreType.DMA((chunks,)),
            pltpu.SemaphoreType.DMA,
        ],
        compiler_params=pltpu.CompilerParams(vmem_limit_bytes=PROJECT_VMEM),
        name="project",
    )(factor_t, attempts)


def add_kernel(in_ref, out_ref, *, parts, copies):
    rows = in_ref.shape[0] // parts
    total = in_ref[:rows, :]
    for part in range(1, parts):
        total = total + in_ref[part * rows : (part + 1) * rows, :]
    for copy in range(copies):
        out_ref[copy * rows : (copy + 1) * rows, :] = total


def add_and_copy(rows, parts, copies, name):
    out_shape = (rows.shape[0] // parts * copies, BLOCK)
    return pl.pallas_call(
        functools.partial(add_kernel, parts=parts, copies=copies),
        in_specs=[VMEM],
        out_specs=VMEM,
        out_shape=jax.ShapeDtypeStruct(out_shape, F32),
        compiler_params=pltpu.CompilerParams(vmem_limit_bytes=max(rows.size, math.prod(out_shape)) * 8 + 1024 * 1024),
        name=name,
    )(rows)


def split(value):
    high = value.astype(BF16)
    return high, (value - high.astype(F32)).astype(BF16)


def right_factor(pair, left_lanes, right_lanes):
    parts = [half * lanes for half in split(pair) for lanes in (left_lanes, right_lanes)]
    return jnp.concatenate(parts, axis=0)


def times(left, right):
    rows = left.shape[0]
    both = jnp.concatenate([jnp.concatenate([half, half], axis=1) for half in split(left)], axis=0)
    product = jnp.dot(both, right, preferred_element_type=F32)
    return product[:rows] + product[rows:]


def solve_kernel(
    raw_ref, core_ref, weights_ref, counts_ref, attempts_ref,
    parts_ref, student_ref, halves, grams, lifts,
):
    count, rank, _ = raw_ref.shape
    students = weights_ref.shape[0]
    wide = students * rank

    ends = [counts_ref[0, 0]]
    for student in range(1, students - 1):
        ends.append(ends[-1] + counts_ref[0, student])
    owners = [sum((block >= end).astype(jnp.int32) for end in ends) for block in range(count)]
    grams[...] = jnp.zeros(grams.shape, F32)
    for block in range(count):
        both = jnp.concatenate(split(raw_ref[block]), axis=0)
        halves[block] = both
        grams[owners[block]] += lax.dot_general(both, both, NT, preferred_element_type=F32)

    lane = lax.broadcasted_iota(jnp.int32, (rank, 2 * rank), 1)
    identity = (lax.broadcasted_iota(jnp.int32, (rank, 2 * rank), 0) == lane % rank).astype(F32)
    on_left = lane[:1] < rank
    left_lanes = (lane < rank).astype(F32).astype(BF16)
    right_lanes = (lane >= rank).astype(F32).astype(BF16)

    def right(pair):
        return right_factor(pair, left_lanes, right_lanes)

    def beside(parts):
        return jnp.concatenate(parts, axis=1)

    core = core_ref[...]
    pairs = range(students // 2)
    scaled = [core * weights_ref[student : student + 1, :] for student in range(students)]
    lift = [beside(scaled[2 * pair : 2 * pair + 2]) for pair in pairs]
    lift_t = [beside([one.T for one in scaled[2 * pair : 2 * pair + 2]]) for pair in pairs]
    lift_right = [right(one) for one in lift]
    lift_t_right = [right(one) for one in lift_t]

    raw_grams = []
    for student in range(students):
        terms = grams[student]
        rows = terms[:rank] + terms[rank:]
        raw_grams.append(rows[:, :rank] + rows[:, rank:])
    raw_right = [right(beside(raw_grams[2 * pair : 2 * pair + 2])) for pair in pairs]
    gram, polynomial = [], []
    for pair in pairs:
        half_way = times(lift[pair], raw_right[pair])
        row = jnp.sum(half_way * lift[pair], axis=0, keepdims=True)
        left_trace = jnp.sum(jnp.where(on_left, row, 0.0), axis=1, keepdims=True)
        right_trace = jnp.sum(jnp.where(on_left, 0.0, row), axis=1, keepdims=True)
        inverse = 1.0 / jnp.sqrt(jnp.where(on_left, left_trace, right_trace) + 1e-06)
        gram.append(times(half_way, lift_t_right[pair]) * (inverse * inverse))
        polynomial.append(lift_t[pair] * inverse)
    for iteration in range(NS_STEPS - 1):
        factor = [1.5 * identity - 0.5 * gram[pair] for pair in pairs]
        factor_right = [right(factor[pair]) for pair in pairs]
        moved = [times(gram[pair], factor_right[pair]) for pair in pairs]
        if iteration < NS_STEPS - 2:
            gram = [times(moved[pair], factor_right[pair]) for pair in pairs]
        polynomial = [times(polynomial[pair], factor_right[pair]) for pair in pairs]
    ahead = [right(times(factor[pair], lift_right[pair])) for pair in pairs]
    bent = [times(polynomial[pair], right(moved[pair])) for pair in pairs]
    straight = [times(polynomial[pair], lift_right[pair]) for pair in pairs]
    apply = beside([1.5 * straight[pair] - 0.5 * times(bent[pair], ahead[pair]) for pair in pairs])
    polynomial = beside([1.5 * polynomial[pair] - 0.5 * times(bent[pair], factor_right[pair]) for pair in pairs])
    for student in range(students):
        high, low = split(apply[:, student * rank : (student + 1) * rank])
        lifts[student] = jnp.concatenate([beside([high, high]), beside([low, low])], axis=0)
    weighted = []
    for block in range(count):
        terms = jnp.dot(lifts[owners[block]], halves[block], preferred_element_type=F32)
        weighted.append((terms[:rank] + terms[rank:]).astype(BF16))
    item_part = jnp.dot(beside(weighted), attempts_ref[...], preferred_element_type=F32)

    turned = beside([polynomial[:, k * rank : (k + 1) * rank].T for k in range(students)])
    crossed = beside([times(turned[:, 2 * pair * rank : 2 * (pair + 1) * rank], raw_right[pair]) for pair in pairs])
    shared = jnp.zeros((rank, rank), F32)
    for student in range(students):
        one = crossed[:, student * rank : (student + 1) * rank]
        shared = shared + one * weights_ref[student : student + 1, :]
        student_ref[student : student + 1, :] = jnp.sum(one * core, axis=0, keepdims=True)

    tiles = item_part.shape[1] // BLOCK
    for tile in range(tiles):
        parts_ref[tile * rank : (tile + 1) * rank, :] = item_part[:, tile * BLOCK : (tile + 1) * BLOCK]
    last = tiles * rank
    parts_ref[last : last + rank // 2, :] = beside([shared[: rank // 2], shared[rank // 2 :]])


def solve(raw, core_factor, student_weights, blocks, attempts, part_rows):
    count, rank, _ = raw.shape
    students = student_weights.shape[0]
    return pl.pallas_call(
        solve_kernel,
        in_specs=[VMEM, VMEM, VMEM, SMEM, VMEM],
        out_specs=[VMEM, VMEM],
        out_shape=[
            jax.ShapeDtypeStruct((part_rows, BLOCK), F32),
            jax.ShapeDtypeStruct((students, rank), F32),
        ],
        scratch_shapes=[
            pltpu.VMEM((count, 2 * rank, BLOCK), BF16),
            pltpu.VMEM((students, 2 * rank, 2 * rank), F32),
            pltpu.VMEM((students, 2 * rank, 2 * rank), BF16),
        ],
        compiler_params=pltpu.CompilerParams(vmem_limit_bytes=16 * 1024 * 1024),
        name="solve",
    )(raw, core_factor, student_weights, blocks, attempts)


def finish_kernel(total_ref, item_ref, shared_ref):
    rank, items = item_ref.shape
    for tile in range(items // BLOCK):
        item_ref[:, tile * BLOCK : (tile + 1) * BLOCK] = total_ref[tile * rank : (tile + 1) * rank, :]
    last = items // BLOCK * rank
    both = total_ref[last : last + rank // 2, :]
    shared_ref[: rank // 2, :] = both[:, :rank]
    shared_ref[rank // 2 :, :] = both[:, rank:]


def finish(total, rank, items):
    return pl.pallas_call(
        finish_kernel,
        in_specs=[VMEM],
        out_specs=[VMEM, VMEM],
        out_shape=[
            jax.ShapeDtypeStruct((rank, items), F32),
            jax.ShapeDtypeStruct((rank, rank), F32),
        ],
        compiler_params=pltpu.CompilerParams(vmem_limit_bytes=2 * 1024 * 1024),
        name="finish",
    )(total)


def exchange(rows, parts, axis, groups=None):
    parted = rows.reshape(parts, -1, 1, BLOCK)
    return lax.all_to_all(parted, axis, 0, 0, tiled=True, axis_index_groups=groups).reshape(rows.shape)


def sum_over(axis, order, rows, gather):
    n_near = len(order)
    near = [[far * n_near + i for i in order] for far in range(N_FAR)]
    distant = [[far * n_near + i for far in (range(N_FAR) if gather else RING)] for i in range(n_near)]
    rows = exchange(rows, n_near, axis, near)
    if gather:
        share = add_and_copy(rows, n_near, 1, "add_near_" + axis)
        rows = lax.all_gather(share, axis, axis_index_groups=distant, tiled=True)
    else:
        rows = exchange(add_and_copy(rows, n_near, N_FAR, "add_near_" + axis), N_FAR, axis, distant)
    return exchange(add_and_copy(rows, N_FAR, n_near, "add_far_" + axis), n_near, axis, near)


def local(n_stu, attempts, item_factor, core_factor, student_weights, blocks):
    items, rank = item_factor.shape
    sums = project(attempts, item_factor.T, 2)
    raw = sum_over("item", NEAR_ITEM, sums.reshape(-1, BLOCK), True).reshape(sums.shape)
    used = items // BLOCK * rank + rank // 2
    parts, student_part = solve(raw, core_factor, student_weights, blocks, attempts, -(-used // n_stu) * n_stu)
    item_total, shared_total = finish(sum_over("stu", NEAR_STU, parts, False), rank, items)
    return (item_total.T, shared_total, student_part)


def solution(mesh):
    in_specs = (P("stu", "item"), P("item", None), P(), P("stu", None), P("stu", None))
    out_specs = (P("item", None), P(), P("stu", None))
    body = functools.partial(local, mesh.shape["stu"])
    return jax.shard_map(body, mesh=mesh, in_specs=in_specs, out_specs=out_specs, check_vma=False)
```
